256 devices in a mesh: illum: 8 (over z), box: 32 (over x, y, core).
Axes of the slice: x: 4, y: 4, z: 8, core: 2. Of those that a mesh axis runs over, the one named last changes fastest.
Arguments:
- patterns: bfloat16 [2, 512, 128, 1024], P(None, 'box', None, 'illum'), parts along dimension 3, may hold values from -6 to 6
- owner_block: int32 [4], replicated, may hold values from 0 to 63
- low_index: int32 [512, 48], P('box'), may hold values from 0 to 315
- low_mask: int32 [512, 48], P('box'), may hold values 0 or 1
- low_table: bfloat16 [2, 316, 128], replicated, may hold values from -2 to 2
- interp: bfloat16 [128, 512], replicated, may hold values from -0.5 to 0.5
- shift_angle: float32 [8, 512], replicated, may hold values from -3.140625 to 3.140625
- par_source: int32 [64, 16], replicated, may hold values from 0 to 63, as said below
- par_index: int32 [64, 16], replicated, may hold values from 0 to 315
- par_mask: int32 [64, 16], replicated, may hold values 0 or 1
- par_table: bfloat16 [2, 316, 512], replicated, may hold values from -1.5 to 1.5
Outputs:
- incoming: float32 [2, 512, 128, 1024], P(None, 'box', None, 'illum'), parts along dimension 3
The draws below stay inside these ranges and needn't reach their ends.
There are 8 independent parts, one for each index of `illum`. The reference program is written for one: setup_inputs(seed, part) draws one part's arguments, and reference() takes and returns one part's arrays. A program takes and returns all parts, laid end to end along the dimension named above; an argument that names none is the same for every part. Nothing has to cross between parts.
Inputs may be any that keep to these rules, and one draw needn't show every extreme that they name: `par_source`: each parent's 16 slots name distinct parents other than itself.
All inputs are finite; a program needn't handle non-finite values. No bound on the sum of `low_mask` on one device may be relied on, other than what follows from the above.
Results may differ from the reference program's by a relative error of at most 0.0047.
Values may be sent and summed in bfloat16 or wider, within the bound.
No kernel may reach another device: no remote copies, remote signals or barrier semaphores. Data moves between devices by JAX's collectives and lax.ppermute only.
A program may use at most 64 MiB of HBM per device.

```python
import jax
import jax.numpy as jnp
from jax import lax

K = 128
Q = 512
R = 128
BOX_DEV = 16
STEPS = 4
NTRANS = 316
PLIST = 16
BOXES = 512
BLOCKS = 64
PARENTS = 64
SRC = 48


def draw_par_source(key, part):
    row_keys = jax.random.split(jax.random.fold_in(key, 7), PARENTS)

    def one_row(row_key):
        rest = jax.random.permutation(row_key, PARENTS - 2).astype(jnp.int32) + 2
        return jnp.concatenate([jnp.ones((1,), jnp.int32), rest[:PLIST - 1]])
    offsets = jax.vmap(one_row)(row_keys)
    base = jnp.arange(PARENTS, dtype=jnp.int32)[:, None]
    return ((base + offsets) % PARENTS).astype(jnp.int32)


def place_ends(array, stream_key, least, top_value):
    longest = array.shape.index(max(array.shape))
    spots = []
    for shift in (0, 1):
        where = [jax.random.randint(jax.random.fold_in(stream_key, axis), (), 0, length) for axis, length in enumerate(array.shape)]
        where[longest] = (where[longest] + shift) % array.shape[longest]
        spots.append(tuple(where))
    return array.at[spots[0]].set(least).at[spots[1]].set(top_value)


def block_scale(rng, dims, pieces, smallest, high):
    def one(axis_at, blocks):
        draws = jax.random.uniform(jax.random.fold_in(jax.random.fold_in(rng, 6), axis_at), (blocks,), jnp.float32, smallest / len(pieces), high / len(pieces))
        return jnp.repeat(jnp.exp(draws), dims[axis_at] // blocks).reshape((-1,) + (1,) * (len(dims) - axis_at - 1))

    factor_of = one(*pieces[0])
    for cut in pieces[1:]:
        factor_of = factor_of * one(*cut)
    return factor_of


def gaussian(rng, shape, width, reach, pieces=(), kind=jnp.bfloat16):
    level = block_scale(rng, shape, pieces, -0.22, 0.18) if pieces else 1.0
    values = jax.random.normal(rng, shape, jnp.float32) * width * level
    return jnp.minimum(jnp.maximum(values, -reach), reach).astype(kind)


def setup_inputs(seed: int = 0, part: int = 0) -> dict:
    key_of = jax.random.split(jax.random.key(seed), 12)
    part_splits = jax.random.split(jax.random.fold_in(key_of[11], part), 12)
    return {
        "patterns": gaussian(part_splits[0], (2, BOXES, K, R), 1.0, 6.0, ((1, 32),)),
        "owner_block": place_ends(jax.random.randint(key_of[1], (STEPS,), 0, BLOCKS), jax.random.fold_in(key_of[1], 1), 0, BLOCKS - 1).astype(jnp.int32),
        "low_index": place_ends(jax.random.randint(key_of[2], (BOXES, SRC), 0, NTRANS), jax.random.fold_in(key_of[2], 1), 0, NTRANS - 1).astype(jnp.int32),
        "low_mask": place_ends((jax.random.randint(key_of[3], (BOXES, SRC), 0, 2) < 1).astype(jnp.int32), jax.random.fold_in(key_of[3], 1), 0, 1),
        "low_table": gaussian(key_of[4], (2, NTRANS, K), 0.15, 2.0),
        "interp": gaussian(key_of[5], (K, Q), K ** -0.5, 0.5),
        "shift_angle": jnp.clip(jax.random.uniform(key_of[6], (8, Q), jnp.float32, -3.140625, 3.140625), -3.140625, 3.140625),
        "par_source": draw_par_source(jax.random.fold_in(key_of[11], 71), part),
        "par_index": place_ends(jax.random.randint(key_of[8], (PARENTS, PLIST), 0, NTRANS), jax.random.fold_in(key_of[8], 1), 0, NTRANS - 1).astype(jnp.int32),
        "par_mask": place_ends((jax.random.randint(key_of[9], (PARENTS, PLIST), 0, 4) < 3).astype(jnp.int32), jax.random.fold_in(key_of[9], 1), 0, 1),
        "par_table": gaussian(key_of[10], (2, NTRANS, Q), 0.1, 1.5),
    }


def complex_apply(operator, sources):
    left_real = operator[0].astype(jnp.float32)
    left_imaginary = operator[1].astype(jnp.float32)
    right_real = sources[0].astype(jnp.float32)
    right_imaginary = sources[1].astype(jnp.float32)
    real_part = jnp.einsum('bjk,jkr->bkr', left_real, right_real) - jnp.einsum('bjk,jkr->bkr', left_imaginary, right_imaginary)
    imaginary = jnp.einsum('bjk,jkr->bkr', left_real, right_imaginary) + jnp.einsum('bjk,jkr->bkr', left_imaginary, right_real)
    return jnp.stack([real_part, imaginary])


def reference(patterns, owner_block, low_index, low_mask, low_table, interp, shift_angle, par_source, par_index, par_mask, par_table):
    boxes = patterns.shape[1]
    clusters = boxes // BOX_DEV
    blocks_each = BOX_DEV // 8
    far_ids = (owner_block[:, None] * 8 + jnp.arange(8, dtype=jnp.int32)[None, :]).reshape(-1).astype(jnp.int32)
    far_patterns = patterns[:, far_ids]
    cosine = jnp.cos(shift_angle)
    sine = jnp.sin(shift_angle)
    interp_wide = interp.astype(jnp.float32)

    def lift_cluster(cluster):
        child = lax.dynamic_slice_in_dim(patterns, cluster * BOX_DEV, BOX_DEV, 1).astype(jnp.float32)
        lifted = jnp.einsum('cbkr,kq->cbqr', child, interp_wide)
        lifted = lifted.reshape(2, blocks_each, 8, Q, R)
        real_part = jnp.sum(cosine[None, :, :, None] * lifted[0] - sine[None, :, :, None] * lifted[1], axis=1)
        imaginary = jnp.sum(cosine[None, :, :, None] * lifted[1] + sine[None, :, :, None] * lifted[0], axis=1)
        return jnp.stack([real_part, imaginary]).astype(jnp.bfloat16)

    lifted_all = lax.map(lift_cluster, jnp.arange(clusters, dtype=jnp.int32))
    parent_patterns = jnp.transpose(lifted_all, (1, 0, 2, 3, 4)).reshape(2, PARENTS, Q, R)

    def add_slot(slot, total):
        source = par_source[:, slot]
        which = par_index[:, slot]
        weight = par_mask[:, slot].astype(jnp.float32)
        picked = parent_patterns[:, source].astype(jnp.float32)
        operator = par_table[:, which].astype(jnp.float32) * weight[None, :, None]
        real_part = operator[0][:, :, None] * picked[0] - operator[1][:, :, None] * picked[1]
        imaginary = operator[0][:, :, None] * picked[1] + operator[1][:, :, None] * picked[0]
        return total + jnp.stack([real_part, imaginary])

    translated = lax.fori_loop(0, PLIST, add_slot, jnp.zeros((2, PARENTS, Q, R), jnp.float32)).astype(jnp.bfloat16)

    def finish_cluster(cluster):
        own = lax.dynamic_slice_in_dim(patterns, cluster * BOX_DEV, BOX_DEV, 1)
        sources = jnp.concatenate([own, far_patterns], axis=1)
        index = lax.dynamic_slice_in_dim(low_index, cluster * BOX_DEV, BOX_DEV, 0)
        keep = lax.dynamic_slice_in_dim(low_mask, cluster * BOX_DEV, BOX_DEV, 0).astype(jnp.float32)
        operator = low_table[:, index].astype(jnp.float32) * keep[None, :, :, None]
        near = complex_apply(jnp.transpose(operator, (0, 1, 2, 3)), sources)
        parents_here = lax.dynamic_slice_in_dim(translated, cluster * blocks_each, blocks_each, 1).astype(jnp.float32)
        wide = parents_here[:, :, None]
        real_part = cosine[None, :, :, None] * wide[0] + sine[None, :, :, None] * wide[1]
        imaginary = cosine[None, :, :, None] * wide[1] - sine[None, :, :, None] * wide[0]
        phased = jnp.stack([real_part, imaginary]).astype(jnp.bfloat16).reshape(2, BOX_DEV, Q, R)
        down = jnp.einsum('cbqr,kq->cbkr', phased.astype(jnp.float32), interp_wide)
        return near + down

    result = lax.map(finish_cluster, jnp.arange(clusters, dtype=jnp.int32))
    return jnp.transpose(result, (1, 0, 2, 3, 4)).reshape(2, boxes, K, R)
```

```python
import jax
import jax.numpy as jnp
from jax import lax
from jax.experimental import pallas as pl
from jax.experimental.pallas import tpu as pltpu
from jax.sharding import PartitionSpec as P

F32 = jnp.float32
BF16 = jnp.bfloat16
LANES = 128
LIMIT = 48 * 1024 * 1024
DEV = 32
BOX = 16
K = 128
Q = 512
R = 128
QS = Q // DEV
KS = K // DEV
NPAD = 384
FAR = 32
L_ROWS = 4 * QS
P_ROWS = 2 * KS * 8
T_ROWS = 2 * BOX
SEND1 = L_ROWS + P_ROWS + T_ROWS
N_ROWS = 2 * KS * BOX
SEND2 = L_ROWS + N_ROWS


def iota(shape, dim):
    return lax.broadcasted_iota(jnp.int32, shape, dim)


def pick(row, index, chunk):
    total = None
    for part in range(NPAD // LANES):
        source = jnp.broadcast_to(row(part), index.shape)
        got = jnp.take_along_axis(source, index, axis=1, mode="promise_in_bounds")
        total = got if total is None else jnp.where(chunk == part, got, total)
    return total


def split(out_ref, c, rows):
    for part in range(NPAD // LANES):
        out_ref[c, part] = rows[:, part * LANES : (part + 1) * LANES]


def transpose_table(table_ref, out_ref):
    count = table_ref.shape[1]
    for part in range(2):
        wide = table_ref[part].astype(F32)
        wide = jnp.concatenate([wide, jnp.zeros((NPAD - count, wide.shape[1]), F32)], axis=0)
        split(out_ref, part, jnp.transpose(wide))


def first_parity(owner, device):
    result = jnp.int32(0)
    for step in reversed(range(owner.shape[0])):
        value = owner[step]
        result = jnp.where((value >> 1) == device, value & 1, result)
    return result


def up_kernel(
    owner, patterns, index, mask, table, interp, angle, send, extra, flag,
    weights, fields, wide, table_t, spread,
):
    me = lax.axis_index("box")
    interp_t = jnp.transpose(interp[...].astype(F32))
    cosine = jnp.transpose(jnp.cos(angle[...]))
    sine = jnp.transpose(jnp.sin(angle[...]))
    for b in range(8):
        rows = 2 * b * K
        weights[:, rows : rows + K] = (interp_t * cosine[:, b : b + 1]).astype(BF16)
        weights[:, rows + K : rows + 2 * K] = (interp_t * sine[:, b : b + 1]).astype(BF16)
        for p in range(2):
            real, imag = patterns[0, 8 * p + b], patterns[1, 8 * p + b]
            fields[rows : rows + K, p * R : (p + 1) * R] = real
            fields[rows + K : rows + 2 * K, p * R : (p + 1) * R] = -imag
            fields[rows : rows + K, (2 + p) * R : (3 + p) * R] = imag
            fields[rows + K : rows + 2 * K, (2 + p) * R : (3 + p) * R] = real
    tile = 128
    for t in range(Q // tile):
        total = jnp.dot(
            weights[t * tile : (t + 1) * tile, :], fields[...], preferred_element_type=F32
        ).astype(BF16)
        ways = tile // QS
        for cp in range(4):
            send[t * ways : (t + 1) * ways, cp * QS : (cp + 1) * QS, :] = total[
                :, cp * R : (cp + 1) * R
            ].reshape(ways, QS, R)

    for c in range(2):
        for b in range(BOX):
            wide[c, b * K : (b + 1) * K, :] = patterns[c, b].astype(F32)
    first = first_parity(owner, me)

    def cut(out, base, parity):
        def one(d, _):
            for c in range(2):
                for half in range(KS // 2):
                    pieces = [
                        wide[c, pl.ds(parity * (8 * K) + d * KS + 2 * half + k, 8, stride=K), :]
                        for k in range(2)
                    ]
                    out[d, base + c * KS * 8 + half * 16 : base + c * KS * 8 + (half + 1) * 16, :] = (
                        jnp.concatenate(pieces, axis=0).astype(BF16)
                    )
            return 0

        lax.fori_loop(0, DEV, one, 0)

    cut(send, L_ROWS, first)
    twice = jnp.int32(0)
    for i in range(owner.shape[0]):
        for j in range(i):
            same = (owner[i] >> 1) == (owner[j] >> 1)
            twice = jnp.where(same & (owner[i] != owner[j]), 1, twice)
    flag[0] = twice

    @pl.when(twice > 0)
    def _():
        cut(extra, 0, 1 - first)

    transpose_table(table, table_t)
    near_count = BOX
    spread[:, 0 : index.shape[1]] = jnp.where(mask[...] > 0, index[...], NPAD - 1)
    lane = iota((BOX, LANES), 1)
    code = jnp.take_along_axis(
        spread[...], near_count + (lane & (FAR - 1)), axis=1, mode="promise_in_bounds"
    )
    low, chunk = code & (LANES - 1), code >> 7

    def operators(d, _):
        for c in range(2):
            total = jnp.zeros((BOX, LANES), F32)
            for k in range(KS):
                got = pick(
                    lambda part: table_t[c, part, pl.ds(d * KS + k, 1), :], low, chunk
                )
                total = jnp.where((lane >> 5) == k, got, total)
            at = L_ROWS + P_ROWS + c * BOX
            send[d, at : at + BOX, :] = total.astype(BF16)
        return 0

    lax.fori_loop(0, DEV, operators, 0)


def side_kernel(
    patterns, index, mask, table, par_source, par_index, par_mask, par_table, near, coupling,
    wide, table_t, par_t, spread, left, right,
):
    me = lax.axis_index("box")
    for c in range(2):
        for b in range(BOX):
            wide[c, b * K : (b + 1) * K, :] = patterns[c, b].astype(F32)
    transpose_table(table, table_t)
    spread[:, 0 : index.shape[1]] = jnp.where(mask[...] > 0, index[...], NPAD - 1)
    lane = iota((BOX, LANES), 1)
    code = jnp.take_along_axis(spread[...], lane & (BOX - 1), axis=1, mode="promise_in_bounds")
    low, chunk = code & (LANES - 1), code >> 7
    imaginary = ((lane >> 4) & 1) == 1
    left[...] = jnp.zeros_like(left)

    def group(g, _):
        for kk in range(8):
            k = g * 8 + kk
            got = [
                pick(lambda part: table_t[c, part, pl.ds(k, 1), :], low, chunk)
                for c in range(2)
            ]
            value = jnp.where(imaginary, got[1], got[0])
            value = jnp.where((lane >> 5) == kk % 4, value, 0.0).astype(BF16)
            at = kk // 4 * LANES
            left[kk * BOX : (kk + 1) * BOX, at : at + LANES] = value
            real = wide[0, pl.ds(k, BOX, stride=K), :]
            imag = wide[1, pl.ds(k, BOX, stride=K), :]
            row = kk * 2 * BOX
            right[row : row + BOX, 0:R] = real.astype(BF16)
            right[row : row + BOX, R : 2 * R] = imag.astype(BF16)
            right[row + BOX : row + 2 * BOX, 0:R] = (-imag).astype(BF16)
            right[row + BOX : row + 2 * BOX, R : 2 * R] = real.astype(BF16)
        total = jnp.dot(left[...], right[...], preferred_element_type=F32)
        for kk in range(8):
            for c in range(2):
                near[c, pl.ds(g * 8 + kk, BOX, stride=K), :] = total[
                    kk * BOX : (kk + 1) * BOX, c * R : (c + 1) * R
                ]
        return 0

    lax.fori_loop(0, K // 8, group, 0)

    chosen = (iota((QS, Q), 1) == me * QS + iota((QS, Q), 0)).astype(BF16)
    count = par_table.shape[1]
    for c in range(2):
        rows = lax.dot_general(
            chosen, par_table[c], (((1,), (1,)), ((), ())), preferred_element_type=F32
        )
        split(par_t, c, jnp.concatenate([rows, jnp.zeros((QS, NPAD - count), F32)], axis=1))
    parents = 2 * DEV
    lanes = iota((parents, LANES), 1)
    source_here = (lanes & (DEV - 1)) * 2 + ((lanes >> 5) & 1)

    def halves(ref):
        return jnp.concatenate([ref[pl.ds(p, DEV, stride=2), :] for p in range(2)], axis=0)

    source, which, used = halves(par_source), halves(par_index), halves(par_mask)
    which = jnp.where(used > 0, which, NPAD - 1)
    table_at = jnp.full((parents, LANES), NPAD - 1, jnp.int32)
    for j in range(source.shape[1]):
        table_at = jnp.where(source[:, j : j + 1] == source_here, which[:, j : j + 1], table_at)
    par_low, par_chunk = table_at & (LANES - 1), table_at >> 7
    par_imaginary = lanes >= parents

    def one_q(q, _):
        got = [
            pick(lambda part: par_t[c, part, pl.ds(q, 1), :], par_low, par_chunk)
            for c in range(2)
        ]
        coupling[q] = jnp.where(par_imaginary, got[1], got[0]).astype(BF16)
        return 0

    lax.fori_loop(0, QS, one_q, 0)


def middle_kernel(owner, received, extra, coupling, send, far, fields, lifted, right, moved):
    for s in range(owner.shape[0]):
        block = owner[s]
        device = block >> 1
        second = (block & 1) != first_parity(owner, device)

        def place(ref, base):
            for c in range(2):
                for half in range(KS // 2):
                    at = base + c * KS * 8 + half * 16
                    piece = ref[device, at : at + 16, :].astype(F32)
                    for k in range(2):
                        row = (2 * half + k) * FAR + s * 8
                        fields[c, row : row + 8, :] = piece[8 * k : 8 * k + 8]

        @pl.when(jnp.logical_not(second))
        def _():
            place(received, L_ROWS)

        @pl.when(second)
        def _():
            place(extra, 0)

    at = L_ROWS + P_ROWS
    operators = jnp.concatenate(
        [received[:, at + c * BOX : at + (c + 1) * BOX, :].reshape(DEV * BOX, LANES) for c in range(2)],
        axis=1,
    )
    far[...] = jnp.zeros_like(far)
    for k in range(KS):
        rows = slice(k * FAR, (k + 1) * FAR)
        under = slice(LANES + k * FAR, LANES + (k + 1) * FAR)
        real, imag = fields[0, rows, :], fields[1, rows, :]
        far[k, rows, 0:R] = real.astype(BF16)
        far[k, rows, R : 2 * R] = imag.astype(BF16)
        far[k, under, 0:R] = (-imag).astype(BF16)
        far[k, under, R : 2 * R] = real.astype(BF16)
    for k in range(KS):
        total = jnp.dot(operators, far[k], preferred_element_type=F32).astype(BF16)
        for c in range(2):
            row = L_ROWS + (c * KS + k) * BOX
            send[:, row : row + BOX, :] = total[:, c * R : (c + 1) * R].reshape(DEV, BOX, R)

    size = DEV * QS
    for cp in range(4):
        lifted[cp * size : (cp + 1) * size, :] = (
            received[:, cp * QS : (cp + 1) * QS, :].reshape(size, R).astype(F32)
        )

    def one_q(q, _):
        parts = [lifted[pl.ds(cp * size + q, DEV, stride=QS), :] for cp in range(4)]
        real = jnp.concatenate(parts[:2], axis=0)
        imag = jnp.concatenate(parts[2:], axis=0)
        right[0 : 2 * DEV, 0:R] = real.astype(BF16)
        right[0 : 2 * DEV, R : 2 * R] = imag.astype(BF16)
        right[2 * DEV : 4 * DEV, 0:R] = (-imag).astype(BF16)
        right[2 * DEV : 4 * DEV, R : 2 * R] = real.astype(BF16)
        total = jnp.dot(coupling[q], right[...], preferred_element_type=F32)
        for c in range(2):
            for p in range(2):
                moved[pl.ds((2 * c + p) * size + q, DEV, stride=QS), :] = total[
                    p * DEV : (p + 1) * DEV, c * R : (c + 1) * R
                ]
        return 0

    lax.fori_loop(0, QS, one_q, 0)
    for cp in range(4):
        send[:, cp * QS : (cp + 1) * QS, :] = (
            moved[cp * size : (cp + 1) * size, :].reshape(DEV, QS, R).astype(BF16)
        )


def down_kernel(received, near, interp, angle, out, fields, far, cosine, sine):
    b = pl.program_id(0)

    @pl.when(b == 0)
    def _():
        cosine[...] = jnp.cos(angle[...])
        sine[...] = jnp.sin(angle[...])
        for p in range(2):
            real = received[:, p * QS : (p + 1) * QS, :].reshape(Q, R)
            imag = received[:, (2 + p) * QS : (3 + p) * QS, :].reshape(Q, R)
            fields[0:Q, p * R : (p + 1) * R] = real
            fields[Q : 2 * Q, p * R : (p + 1) * R] = imag
            fields[0:Q, (2 + p) * R : (3 + p) * R] = imag
            fields[Q : 2 * Q, (2 + p) * R : (3 + p) * R] = -real
        for c in range(2):
            row = L_ROWS + c * KS * BOX
            far[c] = received[:, row : row + KS * BOX, :].reshape(K * BOX, R).astype(F32)

    wide = interp[...].astype(F32)
    weights = jnp.concatenate(
        [
            (wide * cosine[pl.ds(b, 1), :]).astype(BF16),
            (wide * sine[pl.ds(b, 1), :]).astype(BF16),
        ],
        axis=1,
    )
    total = jnp.dot(weights, fields[...], preferred_element_type=F32)
    for c in range(2):
        for p in range(2):
            there = far[c, pl.ds(8 * p + b, K, stride=BOX), :]
            out[c, p, 0] = total[:, (2 * c + p) * R : (2 * c + p + 1) * R] + near[c, p, 0] + there


def in_vmem(count):
    return [pl.BlockSpec(memory_space=pltpu.VMEM)] * count


SCALARS = pl.BlockSpec(memory_space=pltpu.SMEM)


def params():
    return pltpu.CompilerParams(vmem_limit_bytes=LIMIT)


def shards(
    patterns,
    owner_block,
    low_index,
    low_mask,
    low_table,
    interp,
    shift_angle,
    par_source,
    par_index,
    par_mask,
    par_table,
):
    assert patterns.shape == (2, BOX, K, R) and interp.shape == (K, Q)
    assert lax.axis_size("box") == DEV and low_index.shape == (BOX, BOX + FAR)
    send, extra, flag = pl.pallas_call(
        up_kernel,
        out_shape=(
            jax.ShapeDtypeStruct((DEV, SEND1, R), BF16),
            jax.ShapeDtypeStruct((DEV, P_ROWS, R), BF16),
            jax.ShapeDtypeStruct((1,), jnp.int32),
        ),
        in_specs=[SCALARS] + in_vmem(6),
        out_specs=(*in_vmem(2), SCALARS),
        scratch_shapes=[
            pltpu.VMEM((Q, 16 * K), BF16),
            pltpu.VMEM((16 * K, 4 * R), BF16),
            pltpu.VMEM((2, BOX * K, R), F32),
            pltpu.VMEM((2, NPAD // LANES, K, LANES), F32),
            pltpu.VMEM((BOX, LANES), jnp.int32),
        ],
        compiler_params=params(),
        cost_estimate=pl.CostEstimate(
            flops=1200000000, bytes_accessed=4000000, transcendentals=8192
        ),
        name="up",
    )(owner_block, patterns, low_index, low_mask, low_table, interp, shift_angle)

    received = lax.all_to_all(send, "box", split_axis=0, concat_axis=0, tiled=True)

    near, coupling = pl.pallas_call(
        side_kernel,
        out_shape=(
            jax.ShapeDtypeStruct((2, BOX * K, R), F32),
            jax.ShapeDtypeStruct((QS, 2 * DEV, LANES), BF16),
        ),
        in_specs=in_vmem(8),
        out_specs=tuple(in_vmem(2)),
        scratch_shapes=[
            pltpu.VMEM((2, BOX * K, R), F32),
            pltpu.VMEM((2, NPAD // LANES, K, LANES), F32),
            pltpu.VMEM((2, NPAD // LANES, QS, LANES), F32),
            pltpu.VMEM((BOX, LANES), jnp.int32),
            pltpu.VMEM((8 * BOX, 2 * LANES), BF16),
            pltpu.VMEM((2 * LANES, 2 * R), BF16),
        ],
        compiler_params=params(),
        cost_estimate=pl.CostEstimate(
            flops=4000000000, bytes_accessed=12000000, transcendentals=0
        ),
        name="side",
    )(patterns, low_index, low_mask, low_table, par_source, par_index, par_mask, par_table)

    extra = lax.cond(
        flag[0] > 0,
        lambda x: lax.all_to_all(x, "box", split_axis=0, concat_axis=0, tiled=True),
        lambda x: x,
        extra,
    )

    size = DEV * QS
    send = pl.pallas_call(
        middle_kernel,
        out_shape=jax.ShapeDtypeStruct((DEV, SEND2, R), BF16),
        in_specs=[SCALARS] + in_vmem(3),
        out_specs=in_vmem(1)[0],
        scratch_shapes=[
            pltpu.VMEM((KS, 2 * LANES, 2 * R), BF16),
            pltpu.VMEM((2, KS * FAR, R), F32),
            pltpu.VMEM((4 * size, R), F32),
            pltpu.VMEM((4 * DEV, 2 * R), BF16),
            pltpu.VMEM((4 * size, R), F32),
        ],
        compiler_params=params(),
        cost_estimate=pl.CostEstimate(
            flops=800000000, bytes_accessed=4000000, transcendentals=0
        ),
        name="middle",
    )(owner_block, received, extra, coupling)

    received = lax.all_to_all(send, "box", split_axis=0, concat_axis=0, tiled=True)

    block = pl.BlockSpec((2, 2, 1, K, R), lambda b: (0, 0, b, 0, 0))
    whole = [
        pl.BlockSpec(shape, lambda b, n=len(shape): (0,) * n)
        for shape in ((DEV, SEND2, R), (K, Q), (8, Q))
    ]
    out = pl.pallas_call(
        down_kernel,
        grid=(8,),
        out_shape=jax.ShapeDtypeStruct((2, 2, 8, K, R), F32),
        in_specs=[whole[0], block, whole[1], whole[2]],
        out_specs=block,
        scratch_shapes=[
            pltpu.VMEM((2 * Q, 4 * R), BF16),
            pltpu.VMEM((2, K * BOX, R), F32),
            pltpu.VMEM((8, Q), F32),
            pltpu.VMEM((8, Q), F32),
        ],
        compiler_params=params(),
        cost_estimate=pl.CostEstimate(
            flops=1200000000, bytes_accessed=6000000, transcendentals=8192
        ),
        name="down",
    )(received, near.reshape(2, 2, 8, K, R), interp, shift_angle)
    return out.reshape(2, BOX, K, R)


def solution(mesh):
    placed = (
        P(None, "box", None, "illum"),
        P(),
        P("box", None),
        P("box", None),
        P(),
        P(),
        P(),
        P(),
        P(),
        P(),
        P(),
    )
    return jax.shard_map(
        shards, mesh=mesh, in_specs=placed, out_specs=P(None, "box", None, "illum"), check_vma=False
    )
```

```python
import jax
import jax.numpy as jnp
from jax import lax
from jax.experimental import pallas as pl
from jax.experimental.pallas import tpu as pltpu
from jax.sharding import PartitionSpec as P

F32 = jnp.float32
BF16 = jnp.bfloat16
LANES = 128
LIMIT = 40 * 1024 * 1024
FULL = 60 * 1024 * 1024
GROUP = 2
DEV = 32
BOX = 16
K = 128
Q = 512
R = 128
QS = Q // DEV
KS = K // DEV
NPAD = 384
FAR = 32
L_ROWS = 4 * QS
P_ROWS = 2 * KS * 8
T_ROWS = BOX
SEND1 = L_ROWS + P_ROWS + T_ROWS
N_ROWS = 2 * KS * BOX
SEND2 = L_ROWS + N_ROWS


def iota(shape, dim):
    return lax.broadcasted_iota(jnp.int32, shape, dim)


def pick(row, index, chunk):
    total = None
    for part in range(NPAD // LANES):
        source = jnp.broadcast_to(row(part), index.shape)
        got = jnp.take_along_axis(source, index, axis=1, mode="promise_in_bounds")
        total = got if total is None else jnp.where(chunk == part, got, total)
    return total


def split(out_ref, c, rows):
    for part in range(NPAD // LANES):
        out_ref[c, part] = rows[:, part * LANES : (part + 1) * LANES]


def transpose_table(table_ref, out_ref):
    count = table_ref.shape[1]
    for part in range(2):
        wide = table_ref[part].astype(F32)
        wide = jnp.concatenate([wide, jnp.zeros((NPAD - count, wide.shape[1]), F32)], axis=0)
        split(out_ref, part, jnp.transpose(wide))


def first_parity(owner, device):
    result = jnp.int32(0)
    for step in reversed(range(owner.shape[0])):
        value = owner[step]
        result = jnp.where((value >> 1) == device, value & 1, result)
    return result


def widen(patterns, wide, parity):
    for c in range(2):
        for i in range(8):
            wide[c, i * K : (i + 1) * K, :] = patterns[c, parity * 8 + i].astype(F32)


def cut(out, base, wide, devices):
    for d in devices:
        for c in range(2):
            for half in range(KS // 2):
                pieces = [wide[c, pl.ds(d * KS + 2 * half + k, 8, stride=K), :] for k in range(2)]
                at = base + c * KS * 8 + half * 16
                out[d, at : at + 16, :] = jnp.concatenate(pieces, axis=0).astype(BF16)


def start_all(pairs, sems):
    copies = [pltpu.make_async_copy(*pair, sems.at[i]) for i, pair in enumerate(pairs)]
    for copy in copies:
        copy.start()
    return copies


def up_kernel(
    owner_in, patterns_in, index_in, mask_in, interp_in, angle_in, send_out,
    owner, patterns, index, mask, interp, angle, sems, weights, fields, wide, spread, send, out_sems,
):
    copies = start_all(
        (
            (interp_in, interp),
            (angle_in, angle),
            (patterns_in, patterns),
            (owner_in, owner),
            (index_in, index),
            (mask_in, mask),
        ),
        sems,
    )
    me = lax.axis_index("box")
    copies[0].wait()
    copies[1].wait()
    interp_t = jnp.transpose(interp[...].astype(F32))
    cosine = jnp.transpose(jnp.cos(angle[...]))
    sine = jnp.transpose(jnp.sin(angle[...]))
    for b in range(8):
        rows = 2 * b * K
        weights[:, rows : rows + K] = (interp_t * cosine[:, b : b + 1]).astype(BF16)
        weights[:, rows + K : rows + 2 * K] = (interp_t * sine[:, b : b + 1]).astype(BF16)
    for copy in copies[2:]:
        copy.wait()
    for b in range(8):
        rows = 2 * b * K
        for p in range(2):
            real, imag = patterns[0, 8 * p + b], patterns[1, 8 * p + b]
            fields[rows : rows + K, p * R : (p + 1) * R] = real
            fields[rows + K : rows + 2 * K, p * R : (p + 1) * R] = -imag
            fields[rows : rows + K, (2 + p) * R : (3 + p) * R] = imag
            fields[rows + K : rows + 2 * K, (2 + p) * R : (3 + p) * R] = real
    first = first_parity(owner, me)
    widen(patterns, wide, first)

    spread[:, 0 : index.shape[1]] = jnp.where(mask[...] > 0, index[...], NPAD - 1)
    lane = iota((BOX, LANES), 1)
    number = jnp.take_along_axis(
        spread[...], BOX + (lane & (FAR - 1)), axis=1, mode="promise_in_bounds"
    )
    chunk = number >> 7
    scale = jnp.where(chunk == 0, 1.0, jnp.where(chunk == 1, 256.0, 65536.0)).astype(F32)
    code = ((number & (LANES - 1)) + 128).astype(F32) * scale
    quarter = BOX // 4
    packed = code[0:quarter]
    for group in range(1, 4):
        packed = jnp.where(
            lane[0:quarter] >> 5 == group, code[group * quarter : (group + 1) * quarter], packed
        )
    rows = jnp.concatenate([packed] * 4, axis=0).astype(BF16)
    tile = 128
    ways = tile // QS
    outs = []
    for t in range(Q // tile):
        total = jnp.dot(
            weights[t * tile : (t + 1) * tile, :], fields[...], preferred_element_type=F32
        ).astype(BF16)
        here = range(t * ways, (t + 1) * ways)
        cut(send, L_ROWS, wide, here)
        for d in here:
            send[d, L_ROWS + P_ROWS : SEND1, :] = rows
        for cp in range(4):
            send[t * ways : (t + 1) * ways, cp * QS : (cp + 1) * QS, :] = total[
                :, cp * R : (cp + 1) * R
            ].reshape(ways, QS, R)
        piece = pl.ds(t * ways, ways)
        outs.append(pltpu.make_async_copy(send.at[piece], send_out.at[piece], out_sems.at[t]))
        outs[-1].start()
    for copy in outs:
        copy.wait()


def side_kernel(
    owner, patterns_in, index_in, mask_in, table_in, par_source_in, par_index_in, par_mask_in,
    par_table_in, interp_in, angle_in,
    near_out, coupling_out, own_table_out, weights_out, extra_out,
    patterns, index, mask, table, par_source, par_index, par_mask, par_table, interp, angle, sems,
    near, coupling, own_table, weights, extra, out_sems,
    wide, table_t, par_t, spread, par_rows, block,
):
    copies = start_all(
        (
            (table_in, table),
            (par_table_in, par_table),
            (patterns_in, patterns),
            (index_in, index),
            (mask_in, mask),
            (par_source_in, par_source),
            (par_index_in, par_index),
            (par_mask_in, par_mask),
            (interp_in, interp),
            (angle_in, angle),
        ),
        sems,
    )
    me = lax.axis_index("box")
    twice = jnp.int32(0)
    for i in range(owner.shape[0]):
        for j in range(i):
            same = (owner[i] >> 1) == (owner[j] >> 1)
            twice = jnp.where(same & (owner[i] != owner[j]), 1, twice)

    for copy in copies:
        copy.wait()
    transpose_table(table, table_t)
    for c in range(2):
        for part in range(NPAD // LANES):
            for k in range(KS):
                own_table[c, part, k : k + 1, :] = table_t[c, part, pl.ds(me * KS + k, 1), :]

    @pl.when(twice > 0)
    def _():
        widen(patterns, block, 1 - first_parity(owner, me))
        cut(extra, 0, block, range(DEV))
        copy = pltpu.make_async_copy(extra, extra_out, out_sems.at[4])
        copy.start()
        copy.wait()

    chosen = (iota((QS, Q), 1) == me * QS + iota((QS, Q), 0)).astype(BF16)
    count = par_table.shape[1]
    for c in range(2):
        rows = lax.dot_general(
            chosen, par_table[c], (((1,), (1,)), ((), ())), preferred_element_type=F32
        )
        split(par_t, c, jnp.concatenate([rows, jnp.zeros((QS, NPAD - count), F32)], axis=1))
    slots, parents = par_source.shape
    here = iota((LANES, LANES), 0)
    source_here = (here & (DEV - 1)) * 2 + ((here >> 5) & 1)
    par_rows[0, 0:slots, 0:parents] = par_source[...].astype(F32)
    par_rows[1, 0:slots, 0:parents] = jnp.where(
        par_mask[...] > 0, par_index[...], NPAD - 1
    ).astype(F32)
    wanted = source_here.astype(F32)
    table_at = jnp.full((LANES, LANES), NPAD - 1, F32)
    for j in range(slots):
        table_at = jnp.where(
            par_rows[0, j : j + 1, :] == wanted, par_rows[1, j : j + 1, :], table_at
        )
    par_rows[0] = jnp.transpose(table_at)
    number = jnp.concatenate(
        [par_rows[0, pl.ds(p, DEV, stride=2), :] for p in range(2)], axis=0
    ).astype(jnp.int32)
    par_low, par_chunk = number & (LANES - 1), number >> 7
    par_imaginary = iota((parents, LANES), 1) >= parents
    for q in range(QS):
        got = [
            pick(lambda part: par_t[c, part, q : q + 1, :], par_low, par_chunk) for c in range(2)
        ]
        coupling[q] = jnp.where(par_imaginary, got[1], got[0]).astype(BF16)
    outs = start_all(((coupling, coupling_out), (own_table, own_table_out)), out_sems)

    cosine, sine = jnp.cos(angle[...]), jnp.sin(angle[...])
    smooth = interp[...].astype(F32)
    for b in range(8):
        weights[b * K : (b + 1) * K, 0:Q] = (smooth * cosine[b : b + 1, :]).astype(BF16)
        weights[b * K : (b + 1) * K, Q : 2 * Q] = (smooth * sine[b : b + 1, :]).astype(BF16)
    outs.append(pltpu.make_async_copy(weights, weights_out, out_sems.at[2]))
    outs[-1].start()

    for c in range(2):
        for b in range(BOX):
            wide[c, b * K : (b + 1) * K, :] = patterns[c, b].astype(F32)
    spread[:, 0 : index.shape[1]] = jnp.where(mask[...] > 0, index[...], NPAD - 1)
    lane = iota((BOX, LANES), 1)
    code = jnp.take_along_axis(spread[...], lane & (BOX - 1), axis=1, mode="promise_in_bounds")
    low, chunk = code & (LANES - 1), code >> 7
    imaginary = ((lane >> 4) & 1) == 1
    zero = jnp.zeros((BOX, LANES), F32)

    for g in range(K // 8):
        left, right = [], []
        for kk in range(8):
            k = g * 8 + kk
            got = [
                pick(lambda part: table_t[c, part, k : k + 1, :], low, chunk) for c in range(2)
            ]
            value = jnp.where(imaginary, got[1], got[0])
            value = jnp.where((lane >> 5) == kk % 4, value, 0.0)
            left.append(
                jnp.concatenate([value, zero] if kk < 4 else [zero, value], axis=1)
            )
            real, imag = [wide[c, pl.ds(k, BOX, stride=K), :] for c in range(2)]
            right.append(doubled(real, imag))
        total = jnp.dot(
            jnp.concatenate(left, axis=0).astype(BF16),
            jnp.concatenate(right, axis=0),
            preferred_element_type=F32,
        )
        for kk in range(8):
            for c in range(2):
                near[c, pl.ds(g * 8 + kk, BOX, stride=K), :] = total[
                    kk * BOX : (kk + 1) * BOX, c * R : (c + 1) * R
                ]
    outs.append(pltpu.make_async_copy(near, near_out, out_sems.at[3]))
    outs[-1].start()
    for copy in outs:
        copy.wait()


def doubled(real, imag):
    return jnp.concatenate(
        [
            jnp.concatenate([real, imag], axis=1),
            jnp.concatenate([-imag, real], axis=1),
        ],
        axis=0,
    ).astype(BF16)


def middle_kernel(
    owner, received, extra, coupling, table, send,
    sems, fields, lifted, moved, codes, there,
):
    for s in range(owner.shape[0]):
        block = owner[s]
        device = block >> 1
        second = (block & 1) != first_parity(owner, device)

        def put(c, half, piece):
            for k in range(2):
                row = (2 * half + k) * FAR + s * 8
                fields[c, row : row + 8, :] = piece[8 * k : 8 * k + 8].astype(F32)

        for c in range(2):
            for half in range(KS // 2):
                at = c * KS * 8 + half * 16
                put(c, half, received[device, L_ROWS + at : L_ROWS + at + 16, :])

        @pl.when(second)
        def _():
            for c in range(2):
                for half in range(KS // 2):
                    at = c * KS * 8 + half * 16
                    copy = pltpu.make_async_copy(extra.at[device, at : at + 16], there, sems.at[0])
                    copy.start()
                    copy.wait()
                    put(c, half, there[...])

    size = DEV * QS
    for cp in range(4):
        lifted[cp * size : (cp + 1) * size, :] = (
            received[:, cp * QS : (cp + 1) * QS, :].reshape(size, R).astype(F32)
        )
    for q in range(QS):
        parts = [lifted[pl.ds(cp * size + q, DEV, stride=QS), :] for cp in range(4)]
        right = doubled(
            jnp.concatenate(parts[:2], axis=0), jnp.concatenate(parts[2:], axis=0)
        )
        total = jnp.dot(coupling[q], right, preferred_element_type=F32)
        for c in range(2):
            for p in range(2):
                moved[pl.ds((2 * c + p) * size + q, DEV, stride=QS), :] = total[
                    p * DEV : (p + 1) * DEV, c * R : (c + 1) * R
                ]
    for cp in range(4):
        send[:, cp * QS : (cp + 1) * QS, :] = (
            moved[cp * size : (cp + 1) * size, :].reshape(DEV, QS, R).astype(BF16)
        )

    codes[...] = (
        received[:, L_ROWS + P_ROWS : SEND1, :].reshape(DEV * BOX, LANES).astype(F32)
    )
    code = jnp.concatenate([codes[pl.ds(i, DEV, stride=BOX), :] for i in range(4)], axis=0)
    chunk = (code >= 32768.0).astype(jnp.int32) + (code >= 8388608.0).astype(jnp.int32)
    scale = jnp.where(chunk == 0, 1.0, jnp.where(chunk == 1, 1 / 256, 1 / 65536)).astype(F32)
    low = (code * scale).astype(jnp.int32) - 128
    low = low & (LANES - 1)
    lane = iota((4 * DEV, LANES), 1)
    for k in range(KS):
        got = [
            pick(lambda part: table[c, part, k : k + 1, :], low, chunk) for c in range(2)
        ]
        left = jnp.concatenate(
            [
                jnp.concatenate(
                    [jnp.where(lane >> 5 == group, got[c], 0.0) for c in range(2)], axis=1
                ).astype(BF16)
                for group in range(4)
            ],
            axis=0,
        )
        rows = slice(k * FAR, (k + 1) * FAR)
        right = doubled(
            jnp.concatenate([fields[0, rows, :]] * 4, axis=0),
            jnp.concatenate([fields[1, rows, :]] * 4, axis=0),
        )
        total = jnp.dot(left, right, preferred_element_type=F32)
        for c in range(2):
            for b in range(BOX):
                moved[pl.ds((c * KS + k) * size + b, DEV, stride=BOX), :] = total[
                    b * DEV : (b + 1) * DEV, c * R : (c + 1) * R
                ]
    for ck in range(2 * KS):
        row = L_ROWS + ck * BOX
        send[:, row : row + BOX, :] = (
            moved[ck * size : (ck + 1) * size, :].reshape(DEV, BOX, R).astype(BF16)
        )


def down_kernel(received, near, weights, out, fields, far, result, sems):
    for p in range(2):
        real = received[:, p * QS : (p + 1) * QS, :].reshape(Q, R)
        imag = received[:, (2 + p) * QS : (3 + p) * QS, :].reshape(Q, R)
        fields[0:Q, p * R : (p + 1) * R] = real
        fields[Q : 2 * Q, p * R : (p + 1) * R] = imag
        fields[0:Q, (2 + p) * R : (3 + p) * R] = imag
        fields[Q : 2 * Q, (2 + p) * R : (3 + p) * R] = -real
    for c in range(2):
        row = L_ROWS + c * KS * BOX
        far[c] = received[:, row : row + KS * BOX, :].reshape(K * BOX, R).astype(F32)
    copies = []
    for first in range(0, 8, GROUP):
        total = jnp.dot(
            weights[first * K : (first + GROUP) * K, :], fields[...], preferred_element_type=F32
        )
        for p in range(2):
            for b in range(first, first + GROUP):
                box = 8 * p + b
                for c in range(2):
                    there = far[c, pl.ds(box, K, stride=BOX), :]
                    at = (2 * c + p) * R
                    result[c, box] = (
                        total[(b - first) * K : (b - first + 1) * K, at : at + R]
                        + near[c, box * K : (box + 1) * K, :]
                        + there
                    )
        for p in range(2):
            boxes = pl.ds(8 * p + first, GROUP)
            copy = pltpu.make_async_copy(
                result.at[:, boxes], out.at[:, boxes], sems.at[2 * first + p]
            )
            copy.start()
            copies.append(copy)
    for copy in copies:
        copy.wait()


def in_vmem(count):
    return [pl.BlockSpec(memory_space=pltpu.VMEM)] * count


IN_HBM = pl.BlockSpec(memory_space=pltpu.HBM)
SCALARS = pl.BlockSpec(memory_space=pltpu.SMEM)


def anywhere(count):
    return [pl.BlockSpec(memory_space=pl.ANY)] * count


def params(limit):
    return pltpu.CompilerParams(vmem_limit_bytes=limit)


def shards(
    patterns,
    owner_block,
    low_index,
    low_mask,
    low_table,
    interp,
    shift_angle,
    par_source,
    par_index,
    par_mask,
    par_table,
):
    assert patterns.shape == (2, BOX, K, R) and interp.shape == (K, Q)
    assert lax.axis_size("box") == DEV and low_index.shape == (BOX, BOX + FAR)
    send = pl.pallas_call(
        up_kernel,
        out_shape=jax.ShapeDtypeStruct((DEV, SEND1, R), BF16),
        in_specs=anywhere(6),
        out_specs=IN_HBM,
        scratch_shapes=[
            pltpu.SMEM(owner_block.shape, jnp.int32),
            pltpu.VMEM(patterns.shape, BF16),
            pltpu.VMEM(low_index.shape, jnp.int32),
            pltpu.VMEM(low_mask.shape, jnp.int32),
            pltpu.VMEM(interp.shape, BF16),
            pltpu.VMEM(shift_angle.shape, F32),
            pltpu.SemaphoreType.DMA((6,)),
            pltpu.VMEM((Q, 16 * K), BF16),
            pltpu.VMEM((16 * K, 4 * R), BF16),
            pltpu.VMEM((2, 8 * K, R), F32),
            pltpu.VMEM((BOX, LANES), jnp.int32),
            pltpu.VMEM((DEV, SEND1, R), BF16),
            pltpu.SemaphoreType.DMA((5,)),
        ],
        compiler_params=params(FULL),
        cost_estimate=pl.CostEstimate(
            flops=1200000000, bytes_accessed=4000000, transcendentals=8192
        ),
        name="up",
    )(owner_block, patterns, low_index, low_mask, interp, shift_angle)

    received = lax.all_to_all(send, "box", split_axis=0, concat_axis=0, tiled=True)

    made = (
        jax.ShapeDtypeStruct((2, BOX * K, R), F32),
        jax.ShapeDtypeStruct((QS, 2 * DEV, LANES), BF16),
        jax.ShapeDtypeStruct((2, NPAD // LANES, 8, LANES), F32),
        jax.ShapeDtypeStruct((8 * K, 2 * Q), BF16),
        jax.ShapeDtypeStruct((DEV, P_ROWS, R), BF16),
    )
    turned = [jnp.transpose(x) for x in (par_source, par_index, par_mask)]
    near, coupling, own_table, weights, extra = pl.pallas_call(
        side_kernel,
        out_shape=made,
        in_specs=[SCALARS, *anywhere(10)],
        out_specs=(IN_HBM,) * 5,
        scratch_shapes=[
            pltpu.VMEM(patterns.shape, BF16),
            pltpu.VMEM(low_index.shape, jnp.int32),
            pltpu.VMEM(low_mask.shape, jnp.int32),
            pltpu.VMEM(low_table.shape, BF16),
            *[pltpu.VMEM(x.shape, jnp.int32) for x in turned],
            pltpu.VMEM(par_table.shape, BF16),
            pltpu.VMEM(interp.shape, BF16),
            pltpu.VMEM(shift_angle.shape, F32),
            pltpu.SemaphoreType.DMA((10,)),
            *[pltpu.VMEM(x.shape, x.dtype) for x in made],
            pltpu.SemaphoreType.DMA((5,)),
            pltpu.VMEM((2, BOX * K, R), F32),
            pltpu.VMEM((2, NPAD // LANES, K, LANES), F32),
            pltpu.VMEM((2, NPAD // LANES, QS, LANES), F32),
            pltpu.VMEM((BOX, LANES), jnp.int32),
            pltpu.VMEM((2, LANES, LANES), F32),
            pltpu.VMEM((2, 8 * K, R), F32),
        ],
        compiler_params=params(FULL),
        cost_estimate=pl.CostEstimate(
            flops=4000000000, bytes_accessed=12000000, transcendentals=8192
        ),
        name="side",
    )(
        owner_block, patterns, low_index, low_mask, low_table, *turned, par_table, interp,
        shift_angle,
    )

    home, block = owner_block >> 1, owner_block
    twice = jnp.any((home[:, None] == home[None]) & (block[:, None] != block[None]))
    received, extra, twice = lax.optimization_barrier((received, extra, twice))
    extra = lax.cond(
        twice,
        lambda x: lax.all_to_all(x, "box", split_axis=0, concat_axis=0, tiled=True),
        lambda x: x,
        extra,
    )

    size = DEV * QS
    send = pl.pallas_call(
        middle_kernel,
        out_shape=jax.ShapeDtypeStruct((DEV, SEND2, R), BF16),
        in_specs=[SCALARS] + in_vmem(1) + anywhere(1) + in_vmem(2),
        out_specs=in_vmem(1)[0],
        scratch_shapes=[
            pltpu.SemaphoreType.DMA((1,)),
            pltpu.VMEM((2, KS * FAR, R), F32),
            pltpu.VMEM((4 * size, R), F32),
            pltpu.VMEM((2 * KS * size, R), F32),
            pltpu.VMEM((size, LANES), F32),
            pltpu.VMEM((16, R), BF16),
        ],
        compiler_params=params(LIMIT),
        cost_estimate=pl.CostEstimate(
            flops=800000000, bytes_accessed=4000000, transcendentals=0
        ),
        name="middle",
    )(owner_block, received, extra, coupling, own_table)

    received = lax.all_to_all(send, "box", split_axis=0, concat_axis=0, tiled=True)

    return pl.pallas_call(
        down_kernel,
        out_shape=jax.ShapeDtypeStruct((2, BOX, K, R), F32),
        in_specs=in_vmem(3),
        out_specs=IN_HBM,
        scratch_shapes=[
            pltpu.VMEM((2 * Q, 4 * R), BF16),
            pltpu.VMEM((2, K * BOX, R), F32),
            pltpu.VMEM((2, BOX, K, R), F32),
            pltpu.SemaphoreType.DMA((BOX,)),
        ],
        compiler_params=params(LIMIT),
        cost_estimate=pl.CostEstimate(
            flops=1200000000, bytes_accessed=6000000, transcendentals=0
        ),
        name="down",
    )(received, near, weights)


def solution(mesh):
    placed = (
        P(None, "box", None, "illum"),
        P(),
        P("box", None),
        P("box", None),
        P(),
        P(),
        P(),
        P(),
        P(),
        P(),
        P(),
    )
    return jax.shard_map(
        shards, mesh=mesh, in_specs=placed, out_specs=P(None, "box", None, "illum"), check_vma=False
    )
```

```python
import functools

import jax
import jax.numpy as jnp
from jax import lax
from jax.experimental import pallas as pl
from jax.experimental.pallas import tpu as pltpu
from jax.sharding import PartitionSpec as P

F32 = jnp.float32
BF16 = jnp.bfloat16
LANES = 128
LIMIT = 40 * 1024 * 1024
FULL = 60 * 1024 * 1024
GROUP = 2
DEV = 32
BOX = 16
K = 128
Q = 512
R = 128
QS = Q // DEV
KS = K // DEV
NPAD = 384
FAR = 32
L_ROWS = 4 * QS
P_ROWS = 2 * KS * 8
T_ROWS = BOX
SEND1 = L_ROWS + P_ROWS + T_ROWS
N_ROWS = 2 * KS * BOX
SEND2 = L_ROWS + N_ROWS


def iota(shape, dim):
    return lax.broadcasted_iota(jnp.int32, shape, dim)


def pick(row, index, chunk):
    total = None
    for part in range(NPAD // LANES):
        source = jnp.broadcast_to(row(part), index.shape)
        got = jnp.take_along_axis(source, index, axis=1, mode="promise_in_bounds")
        total = got if total is None else jnp.where(chunk == part, got, total)
    return total


def split(out_ref, c, rows):
    for part in range(NPAD // LANES):
        out_ref[c, part] = rows[:, part * LANES : (part + 1) * LANES]


def transpose_table(table_ref, out_ref):
    count = table_ref.shape[1]
    for part in range(2):
        wide = table_ref[part].astype(F32)
        wide = jnp.concatenate([wide, jnp.zeros((NPAD - count, wide.shape[1]), F32)], axis=0)
        split(out_ref, part, jnp.transpose(wide))


def first_parity(owner, device):
    result = jnp.int32(0)
    for step in reversed(range(owner.shape[0])):
        value = owner[step]
        result = jnp.where((value >> 1) == device, value & 1, result)
    return result


def widen(patterns, wide, parity):
    for c in range(2):
        for i in range(8):
            wide[c, i * K : (i + 1) * K, :] = patterns[c, parity * 8 + i].astype(F32)


def cut(out, base, wide, devices):
    for d in devices:
        for c in range(2):
            for half in range(KS // 2):
                pieces = [wide[c, pl.ds(d * KS + 2 * half + k, 8, stride=K), :] for k in range(2)]
                at = base + c * KS * 8 + half * 16
                out[d, at : at + 16, :] = jnp.concatenate(pieces, axis=0).astype(BF16)


def start_all(pairs, sems):
    copies = [pltpu.make_async_copy(*pair, sems.at[i]) for i, pair in enumerate(pairs)]
    for copy in copies:
        copy.start()
    return copies


def up_kernel(
    owner_in, patterns_in, index_in, mask_in, interp_in, angle_in, send_out,
    owner, patterns, index, mask, interp, angle, sems, weights, fields, wide, spread, send, out_sems,
):
    copies = start_all(
        (
            (interp_in, interp),
            (angle_in, angle),
            (patterns_in, patterns),
            (owner_in, owner),
            (index_in, index),
            (mask_in, mask),
        ),
        sems,
    )
    me = lax.axis_index("box")
    copies[0].wait()
    copies[1].wait()
    smooth = interp[...].astype(F32)
    cosine, sine = jnp.cos(angle[...]), jnp.sin(angle[...])
    for b in range(8):
        rows = 2 * b * K
        weights[rows : rows + K, :] = (smooth * cosine[b : b + 1, :]).astype(BF16)
        weights[rows + K : rows + 2 * K, :] = (smooth * sine[b : b + 1, :]).astype(BF16)
    for copy in copies[2:]:
        copy.wait()
    for b in range(8):
        rows = 2 * b * K
        for p in range(2):
            real, imag = patterns[0, 8 * p + b], patterns[1, 8 * p + b]
            fields[rows : rows + K, p * R : (p + 1) * R] = real
            fields[rows + K : rows + 2 * K, p * R : (p + 1) * R] = -imag
            fields[rows : rows + K, (2 + p) * R : (3 + p) * R] = imag
            fields[rows + K : rows + 2 * K, (2 + p) * R : (3 + p) * R] = real
    first = first_parity(owner, me)
    widen(patterns, wide, first)

    spread[:, 0 : index.shape[1]] = jnp.where(mask[...] > 0, index[...], NPAD - 1)
    lane = iota((BOX, LANES), 1)
    number = jnp.take_along_axis(
        spread[...], BOX + (lane & (FAR - 1)), axis=1, mode="promise_in_bounds"
    )
    chunk = number >> 7
    scale = jnp.where(chunk == 0, 1.0, jnp.where(chunk == 1, 256.0, 65536.0)).astype(F32)
    code = ((number & (LANES - 1)) + 128).astype(F32) * scale
    quarter = BOX // 4
    packed = code[0:quarter]
    for group in range(1, 4):
        packed = jnp.where(
            lane[0:quarter] >> 5 == group, code[group * quarter : (group + 1) * quarter], packed
        )
    rows = jnp.concatenate([packed] * 4, axis=0).astype(BF16)
    tile = 256
    ways = tile // QS
    outs = []
    for t in range(Q // tile):
        total = lax.dot_general(
            weights[:, t * tile : (t + 1) * tile],
            fields[...],
            (((0,), (0,)), ((), ())),
            preferred_element_type=F32,
        ).astype(BF16)
        here = range(t * ways, (t + 1) * ways)
        cut(send, L_ROWS, wide, here)
        for d in here:
            send[d, L_ROWS + P_ROWS : SEND1, :] = rows
        for cp in range(4):
            send[t * ways : (t + 1) * ways, cp * QS : (cp + 1) * QS, :] = total[
                :, cp * R : (cp + 1) * R
            ].reshape(ways, QS, R)
        piece = pl.ds(t * ways, ways)
        outs.append(pltpu.make_async_copy(send.at[piece], send_out.at[piece], out_sems.at[t]))
        outs[-1].start()
    for copy in outs:
        copy.wait()


def side_kernel(
    owner, patterns_in, index_in, mask_in, table_in, par_source_in, par_index_in, par_mask_in,
    par_table_in, interp_in, angle_in,
    near_out, coupling_out, own_table_out, weights_out, extra_out,
    patterns, index, mask, table, par_source, par_index, par_mask, par_table, interp, angle, sems,
    near, coupling, own_table, weights, extra, out_sems,
    wide, table_t, par_t, spread, par_rows, block,
):
    copies = start_all(
        (
            (table_in, table),
            (par_table_in, par_table),
            (patterns_in, patterns),
            (index_in, index),
            (mask_in, mask),
            (par_source_in, par_source),
            (par_index_in, par_index),
            (par_mask_in, par_mask),
            (interp_in, interp),
            (angle_in, angle),
        ),
        sems,
    )
    me = lax.axis_index("box")
    twice = jnp.int32(0)
    for i in range(owner.shape[0]):
        for j in range(i):
            same = (owner[i] >> 1) == (owner[j] >> 1)
            twice = jnp.where(same & (owner[i] != owner[j]), 1, twice)

    for copy in copies:
        copy.wait()
    transpose_table(table, table_t)
    for c in range(2):
        for part in range(NPAD // LANES):
            for k in range(KS):
                own_table[c, part, k : k + 1, :] = table_t[c, part, pl.ds(me * KS + k, 1), :]

    @pl.when(twice > 0)
    def _():
        widen(patterns, block, 1 - first_parity(owner, me))
        cut(extra, 0, block, range(DEV))
        copy = pltpu.make_async_copy(extra, extra_out, out_sems.at[4])
        copy.start()
        copy.wait()

    chosen = (iota((QS, Q), 1) == me * QS + iota((QS, Q), 0)).astype(BF16)
    count = par_table.shape[1]
    for c in range(2):
        rows = lax.dot_general(
            chosen, par_table[c], (((1,), (1,)), ((), ())), preferred_element_type=F32
        )
        split(par_t, c, jnp.concatenate([rows, jnp.zeros((QS, NPAD - count), F32)], axis=1))
    slots, parents = par_source.shape
    here = iota((LANES, LANES), 0)
    source_here = (here & (DEV - 1)) * 2 + ((here >> 5) & 1)
    par_rows[0, 0:slots, 0:parents] = par_source[...].astype(F32)
    par_rows[1, 0:slots, 0:parents] = jnp.where(
        par_mask[...] > 0, par_index[...], NPAD - 1
    ).astype(F32)
    wanted = source_here.astype(F32)
    table_at = jnp.full((LANES, LANES), NPAD - 1, F32)
    for j in range(slots):
        table_at = jnp.where(
            par_rows[0, j : j + 1, :] == wanted, par_rows[1, j : j + 1, :], table_at
        )
    par_rows[0] = jnp.transpose(table_at)
    number = jnp.concatenate(
        [par_rows[0, pl.ds(p, DEV, stride=2), :] for p in range(2)], axis=0
    ).astype(jnp.int32)
    par_low, par_chunk = number & (LANES - 1), number >> 7
    par_imaginary = iota((parents, LANES), 1) >= parents
    for q in range(QS):
        got = [
            pick(lambda part: par_t[c, part, q : q + 1, :], par_low, par_chunk) for c in range(2)
        ]
        coupling[q] = jnp.where(par_imaginary, got[1], got[0]).astype(BF16)
    outs = start_all(((coupling, coupling_out), (own_table, own_table_out)), out_sems)

    cosine, sine = jnp.cos(angle[...]), jnp.sin(angle[...])
    smooth = interp[...].astype(F32)
    for b in range(8):
        weights[b * K : (b + 1) * K, 0:Q] = (smooth * cosine[b : b + 1, :]).astype(BF16)
        weights[b * K : (b + 1) * K, Q : 2 * Q] = (smooth * sine[b : b + 1, :]).astype(BF16)
    outs.append(pltpu.make_async_copy(weights, weights_out, out_sems.at[2]))
    outs[-1].start()

    for c in range(2):
        for b in range(BOX):
            wide[c, b * K : (b + 1) * K, :] = patterns[c, b].astype(F32)
    spread[:, 0 : index.shape[1]] = jnp.where(mask[...] > 0, index[...], NPAD - 1)
    lane = iota((BOX, LANES), 1)
    code = jnp.take_along_axis(spread[...], lane & (BOX - 1), axis=1, mode="promise_in_bounds")
    low, chunk = code & (LANES - 1), code >> 7
    imaginary = ((lane >> 4) & 1) == 1
    zero = jnp.zeros((BOX, LANES), F32)

    for g in range(K // 8):
        left, right = [], []
        for kk in range(8):
            k = g * 8 + kk
            got = [
                pick(lambda part: table_t[c, part, k : k + 1, :], low, chunk) for c in range(2)
            ]
            value = jnp.where(imaginary, got[1], got[0])
            value = jnp.where((lane >> 5) == kk % 4, value, 0.0)
            left.append(
                jnp.concatenate([value, zero] if kk < 4 else [zero, value], axis=1)
            )
            real, imag = [wide[c, pl.ds(k, BOX, stride=K), :] for c in range(2)]
            right.append(doubled(real, imag))
        total = jnp.dot(
            jnp.concatenate(left, axis=0).astype(BF16),
            jnp.concatenate(right, axis=0),
            preferred_element_type=F32,
        )
        for kk in range(8):
            for c in range(2):
                near[c, pl.ds(g * 8 + kk, BOX, stride=K), :] = total[
                    kk * BOX : (kk + 1) * BOX, c * R : (c + 1) * R
                ]
    outs.append(pltpu.make_async_copy(near, near_out, out_sems.at[3]))
    outs[-1].start()
    for copy in outs:
        copy.wait()


def doubled(real, imag):
    return jnp.concatenate(
        [
            jnp.concatenate([real, imag], axis=1),
            jnp.concatenate([-imag, real], axis=1),
        ],
        axis=0,
    ).astype(BF16)


def middle_kernel(
    owner, received, extra, coupling, table, send,
    sems, fields, lifted, moved, codes, there,
):
    def place(s, c, half, piece):
        for k in range(2):
            row = (2 * half + k) * FAR + s * 8
            fields[c, row : row + 8, :] = piece[8 * k : 8 * k + 8].astype(F32)

    pieces = [
        (c, half, c * KS * 8 + half * 16) for c in range(2) for half in range(KS // 2)
    ]
    seconds = []
    for s in range(owner.shape[0]):
        device = owner[s] >> 1
        seconds.append((owner[s] & 1) != first_parity(owner, device))
        for c, half, at in pieces:
            place(s, c, half, received[device, L_ROWS + at : L_ROWS + at + 16, :])

    @pl.when(functools.reduce(jnp.logical_or, seconds))
    def _():
        for s, second in enumerate(seconds):

            @pl.when(second)
            def _():
                for c, half, at in pieces:
                    copy = pltpu.make_async_copy(
                        extra.at[owner[s] >> 1, at : at + 16], there, sems.at[0]
                    )
                    copy.start()
                    copy.wait()
                    place(s, c, half, there[...])

    size = DEV * QS
    for cp in range(4):
        lifted[cp * size : (cp + 1) * size, :] = (
            received[:, cp * QS : (cp + 1) * QS, :].reshape(size, R).astype(F32)
        )
    for q in range(QS):
        parts = [lifted[pl.ds(cp * size + q, DEV, stride=QS), :] for cp in range(4)]
        right = doubled(
            jnp.concatenate(parts[:2], axis=0), jnp.concatenate(parts[2:], axis=0)
        )
        total = jnp.dot(coupling[q], right, preferred_element_type=F32)
        for c in range(2):
            for p in range(2):
                moved[pl.ds((2 * c + p) * size + q, DEV, stride=QS), :] = total[
                    p * DEV : (p + 1) * DEV, c * R : (c + 1) * R
                ]
    for cp in range(4):
        send[:, cp * QS : (cp + 1) * QS, :] = (
            moved[cp * size : (cp + 1) * size, :].reshape(DEV, QS, R).astype(BF16)
        )

    codes[...] = (
        received[:, L_ROWS + P_ROWS : SEND1, :].reshape(DEV * BOX, LANES).astype(F32)
    )
    code = jnp.concatenate([codes[pl.ds(i, DEV, stride=BOX), :] for i in range(4)], axis=0)
    chunk = (code >= 32768.0).astype(jnp.int32) + (code >= 8388608.0).astype(jnp.int32)
    scale = jnp.where(chunk == 0, 1.0, jnp.where(chunk == 1, 1 / 256, 1 / 65536)).astype(F32)
    low = (code * scale).astype(jnp.int32) - 128
    low = low & (LANES - 1)
    lane = iota((4 * DEV, 2 * LANES), 1) & (LANES - 1)
    keeps = [jnp.where(lane >> 5 == group, 1.0, 0.0).astype(BF16) for group in range(4)]
    for k in range(KS):
        got = [
            pick(lambda part: table[c, part, k : k + 1, :], low, chunk) for c in range(2)
        ]
        both = jnp.concatenate(got, axis=1).astype(BF16)
        left = jnp.concatenate([both * keep for keep in keeps], axis=0)
        rows = slice(k * FAR, (k + 1) * FAR)
        right = doubled(
            jnp.concatenate([fields[0, rows, :]] * 4, axis=0),
            jnp.concatenate([fields[1, rows, :]] * 4, axis=0),
        )
        total = jnp.dot(left, right, preferred_element_type=F32)
        for c in range(2):
            for b in range(BOX):
                moved[pl.ds((c * KS + k) * size + b, DEV, stride=BOX), :] = total[
                    b * DEV : (b + 1) * DEV, c * R : (c + 1) * R
                ]
    for ck in range(2 * KS):
        row = L_ROWS + ck * BOX
        send[:, row : row + BOX, :] = (
            moved[ck * size : (ck + 1) * size, :].reshape(DEV, BOX, R).astype(BF16)
        )


def down_kernel(received, near, weights, out, fields, far, result, sems):
    for p in range(2):
        real = received[:, p * QS : (p + 1) * QS, :].reshape(Q, R)
        imag = received[:, (2 + p) * QS : (3 + p) * QS, :].reshape(Q, R)
        fields[0:Q, p * R : (p + 1) * R] = real
        fields[Q : 2 * Q, p * R : (p + 1) * R] = imag
        fields[0:Q, (2 + p) * R : (3 + p) * R] = imag
        fields[Q : 2 * Q, (2 + p) * R : (3 + p) * R] = -real
    for c in range(2):
        row = L_ROWS + c * KS * BOX
        far[c] = received[:, row : row + KS * BOX, :].reshape(K * BOX, R).astype(F32)
    copies = []
    for first in range(0, 8, GROUP):
        total = jnp.dot(
            weights[first * K : (first + GROUP) * K, :], fields[...], preferred_element_type=F32
        )
        for p in range(2):
            for b in range(first, first + GROUP):
                box = 8 * p + b
                for c in range(2):
                    there = far[c, pl.ds(box, K, stride=BOX), :]
                    at = (2 * c + p) * R
                    result[c, box] = (
                        total[(b - first) * K : (b - first + 1) * K, at : at + R]
                        + near[c, box * K : (box + 1) * K, :]
                        + there
                    )
        for p in range(2):
            boxes = pl.ds(8 * p + first, GROUP)
            copy = pltpu.make_async_copy(
                result.at[:, boxes], out.at[:, boxes], sems.at[2 * first + p]
            )
            copy.start()
            copies.append(copy)
    for copy in copies:
        copy.wait()


def in_vmem(count):
    return [pl.BlockSpec(memory_space=pltpu.VMEM)] * count


IN_HBM = pl.BlockSpec(memory_space=pltpu.HBM)
SCALARS = pl.BlockSpec(memory_space=pltpu.SMEM)


def anywhere(count):
    return [pl.BlockSpec(memory_space=pl.ANY)] * count


def params(limit):
    return pltpu.CompilerParams(vmem_limit_bytes=limit)


def shards(
    patterns,
    owner_block,
    low_index,
    low_mask,
    low_table,
    interp,
    shift_angle,
    par_source,
    par_index,
    par_mask,
    par_table,
):
    assert patterns.shape == (2, BOX, K, R) and interp.shape == (K, Q)
    assert lax.axis_size("box") == DEV and low_index.shape == (BOX, BOX + FAR)
    send = pl.pallas_call(
        up_kernel,
        out_shape=jax.ShapeDtypeStruct((DEV, SEND1, R), BF16),
        in_specs=anywhere(6),
        out_specs=IN_HBM,
        scratch_shapes=[
            pltpu.SMEM(owner_block.shape, jnp.int32),
            pltpu.VMEM(patterns.shape, BF16),
            pltpu.VMEM(low_index.shape, jnp.int32),
            pltpu.VMEM(low_mask.shape, jnp.int32),
            pltpu.VMEM(interp.shape, BF16),
            pltpu.VMEM(shift_angle.shape, F32),
            pltpu.SemaphoreType.DMA((6,)),
            pltpu.VMEM((16 * K, Q), BF16),
            pltpu.VMEM((16 * K, 4 * R), BF16),
            pltpu.VMEM((2, 8 * K, R), F32),
            pltpu.VMEM((BOX, LANES), jnp.int32),
            pltpu.VMEM((DEV, SEND1, R), BF16),
            pltpu.SemaphoreType.DMA((5,)),
        ],
        compiler_params=params(FULL),
        cost_estimate=pl.CostEstimate(
            flops=1200000000, bytes_accessed=4000000, transcendentals=8192
        ),
        name="up",
    )(owner_block, patterns, low_index, low_mask, interp, shift_angle)

    received = lax.all_to_all(send, "box", split_axis=0, concat_axis=0, tiled=True)

    made = (
        jax.ShapeDtypeStruct((2, BOX * K, R), F32),
        jax.ShapeDtypeStruct((QS, 2 * DEV, LANES), BF16),
        jax.ShapeDtypeStruct((2, NPAD // LANES, 8, LANES), F32),
        jax.ShapeDtypeStruct((8 * K, 2 * Q), BF16),
        jax.ShapeDtypeStruct((DEV, P_ROWS, R), BF16),
    )
    turned = [jnp.transpose(x) for x in (par_source, par_index, par_mask)]
    near, coupling, own_table, weights, extra = pl.pallas_call(
        side_kernel,
        out_shape=made,
        in_specs=[SCALARS, *anywhere(10)],
        out_specs=(IN_HBM,) * 5,
        scratch_shapes=[
            pltpu.VMEM(patterns.shape, BF16),
            pltpu.VMEM(low_index.shape, jnp.int32),
            pltpu.VMEM(low_mask.shape, jnp.int32),
            pltpu.VMEM(low_table.shape, BF16),
            *[pltpu.VMEM(x.shape, jnp.int32) for x in turned],
            pltpu.VMEM(par_table.shape, BF16),
            pltpu.VMEM(interp.shape, BF16),
            pltpu.VMEM(shift_angle.shape, F32),
            pltpu.SemaphoreType.DMA((10,)),
            *[pltpu.VMEM(x.shape, x.dtype) for x in made],
            pltpu.SemaphoreType.DMA((5,)),
            pltpu.VMEM((2, BOX * K, R), F32),
            pltpu.VMEM((2, NPAD // LANES, K, LANES), F32),
            pltpu.VMEM((2, NPAD // LANES, QS, LANES), F32),
            pltpu.VMEM((BOX, LANES), jnp.int32),
            pltpu.VMEM((2, LANES, LANES), F32),
            pltpu.VMEM((2, 8 * K, R), F32),
        ],
        compiler_params=params(FULL),
        cost_estimate=pl.CostEstimate(
            flops=4000000000, bytes_accessed=12000000, transcendentals=8192
        ),
        name="side",
    )(
        owner_block, patterns, low_index, low_mask, low_table, *turned, par_table, interp,
        shift_angle,
    )

    home, block = owner_block >> 1, owner_block
    twice = jnp.any((home[:, None] == home[None]) & (block[:, None] != block[None]))
    received, extra, twice = lax.optimization_barrier((received, extra, twice))
    extra = lax.cond(
        twice,
        lambda x: lax.all_to_all(x, "box", split_axis=0, concat_axis=0, tiled=True),
        lambda x: x,
        extra,
    )

    size = DEV * QS
    send = pl.pallas_call(
        middle_kernel,
        out_shape=jax.ShapeDtypeStruct((DEV, SEND2, R), BF16),
        in_specs=[SCALARS] + in_vmem(1) + anywhere(1) + in_vmem(2),
        out_specs=in_vmem(1)[0],
        scratch_shapes=[
            pltpu.SemaphoreType.DMA((1,)),
            pltpu.VMEM((2, KS * FAR, R), F32),
            pltpu.VMEM((4 * size, R), F32),
            pltpu.VMEM((2 * KS * size, R), F32),
            pltpu.VMEM((size, LANES), F32),
            pltpu.VMEM((16, R), BF16),
        ],
        compiler_params=params(LIMIT),
        cost_estimate=pl.CostEstimate(
            flops=800000000, bytes_accessed=4000000, transcendentals=0
        ),
        name="middle",
    )(owner_block, received, extra, coupling, own_table)

    received = lax.all_to_all(send, "box", split_axis=0, concat_axis=0, tiled=True)

    return pl.pallas_call(
        down_kernel,
        out_shape=jax.ShapeDtypeStruct((2, BOX, K, R), F32),
        in_specs=in_vmem(3),
        out_specs=IN_HBM,
        scratch_shapes=[
            pltpu.VMEM((2 * Q, 4 * R), BF16),
            pltpu.VMEM((2, K * BOX, R), F32),
            pltpu.VMEM((2, BOX, K, R), F32),
            pltpu.SemaphoreType.DMA((BOX,)),
        ],
        compiler_params=params(LIMIT),
        cost_estimate=pl.CostEstimate(
            flops=1200000000, bytes_accessed=6000000, transcendentals=0
        ),
        name="down",
    )(received, near, weights)


def solution(mesh):
    placed = (
        P(None, "box", None, "illum"),
        P(),
        P("box", None),
        P("box", None),
        P(),
        P(),
        P(),
        P(),
        P(),
        P(),
        P(),
    )
    return jax.shard_map(
        shards, mesh=mesh, in_specs=placed, out_specs=P(None, "box", None, "illum"), check_vma=False
    )
```

```python
import functools

import jax
import jax.numpy as jnp
from jax import lax
from jax.experimental import pallas as pl
from jax.experimental.pallas import tpu as pltpu
from jax.sharding import PartitionSpec as P

F32 = jnp.float32
BF16 = jnp.bfloat16
LANES = 128
LIMIT = 40 * 1024 * 1024
FULL = 60 * 1024 * 1024
GROUP = 2
DEV = 32
BOX = 16
K = 128
Q = 512
R = 128
QS = Q // DEV
KS = K // DEV
NPAD = 384
FAR = 32
L_ROWS = 4 * QS
P_ROWS = 2 * KS * 8
T_ROWS = BOX
SEND1 = L_ROWS + P_ROWS + T_ROWS
N_ROWS = 2 * KS * BOX
SEND2 = L_ROWS + N_ROWS


def iota(shape, dim):
    return lax.broadcasted_iota(jnp.int32, shape, dim)


def pick(row, index, chunk):
    total = None
    for part in range(NPAD // LANES):
        source = jnp.broadcast_to(row(part), index.shape)
        got = jnp.take_along_axis(source, index, axis=1, mode="promise_in_bounds")
        total = got if total is None else jnp.where(chunk == part, got, total)
    return total


def split(out_ref, c, rows):
    for part in range(NPAD // LANES):
        out_ref[c, part] = rows[:, part * LANES : (part + 1) * LANES]


def transpose_table(table_ref, out_ref):
    count = table_ref.shape[1]
    for part in range(2):
        wide = table_ref[part].astype(F32)
        wide = jnp.concatenate([wide, jnp.zeros((NPAD - count, wide.shape[1]), F32)], axis=0)
        split(out_ref, part, jnp.transpose(wide))


def first_parity(owner, device):
    result = jnp.int32(0)
    for step in reversed(range(owner.shape[0])):
        value = owner[step]
        result = jnp.where((value >> 1) == device, value & 1, result)
    return result


def widen(patterns, wide, parity):
    for c in range(2):
        for i in range(8):
            wide[c, i * K : (i + 1) * K, :] = patterns[c, parity * 8 + i].astype(F32)


def cut(out, base, wide, devices):
    for d in devices:
        for c in range(2):
            for half in range(KS // 2):
                pieces = [wide[c, pl.ds(d * KS + 2 * half + k, 8, stride=K), :] for k in range(2)]
                at = base + c * KS * 8 + half * 16
                out[d, at : at + 16, :] = jnp.concatenate(pieces, axis=0).astype(BF16)


def start_all(pairs, sems):
    copies = [pltpu.make_async_copy(*pair, sems.at[i]) for i, pair in enumerate(pairs)]
    for copy in copies:
        copy.start()
    return copies


def up_kernel(
    owner_in, patterns_in, index_in, mask_in, interp_in, angle_in, send_out,
    owner, patterns, index, mask, interp, angle, sems, weights, fields, wide, spread, send, out_sems,
):
    copies = start_all(
        (
            (interp_in, interp),
            (angle_in, angle),
            (patterns_in, patterns),
            (owner_in, owner),
            (index_in, index),
            (mask_in, mask),
        ),
        sems,
    )
    me = lax.axis_index("box")
    copies[0].wait()
    copies[1].wait()
    smooth = interp[...].astype(F32)
    cosine, sine = jnp.cos(angle[...]), jnp.sin(angle[...])
    for b in range(8):
        rows = 2 * b * K
        weights[rows : rows + K, :] = (smooth * cosine[b : b + 1, :]).astype(BF16)
        weights[rows + K : rows + 2 * K, :] = (smooth * sine[b : b + 1, :]).astype(BF16)
    for copy in copies[2:]:
        copy.wait()
    for b in range(8):
        rows = 2 * b * K
        for p in range(2):
            real, imag = patterns[0, 8 * p + b], patterns[1, 8 * p + b]
            fields[rows : rows + K, p * R : (p + 1) * R] = real
            fields[rows + K : rows + 2 * K, p * R : (p + 1) * R] = -imag
            fields[rows : rows + K, (2 + p) * R : (3 + p) * R] = imag
            fields[rows + K : rows + 2 * K, (2 + p) * R : (3 + p) * R] = real
    first = first_parity(owner, me)
    spread[:, 0 : index.shape[1]] = jnp.where(mask[...] > 0, index[...], NPAD - 1)
    lane = iota((BOX, LANES), 1)
    number = jnp.take_along_axis(
        spread[...], BOX + (lane & (FAR - 1)), axis=1, mode="promise_in_bounds"
    )
    chunk = number >> 7
    scale = jnp.where(chunk == 0, 1.0, jnp.where(chunk == 1, 256.0, 65536.0)).astype(F32)
    code = ((number & (LANES - 1)) + 128).astype(F32) * scale
    quarter = BOX // 4
    packed = code[0:quarter]
    for group in range(1, 4):
        packed = jnp.where(
            lane[0:quarter] >> 5 == group, code[group * quarter : (group + 1) * quarter], packed
        )
    rows = jnp.concatenate([packed] * 4, axis=0).astype(BF16)
    tile = 256
    ways = tile // QS
    outs = []
    for t in range(Q // tile):
        total = lax.dot_general(
            weights[:, t * tile : (t + 1) * tile],
            fields[...],
            (((0,), (0,)), ((), ())),
            preferred_element_type=F32,
        ).astype(BF16)
        here = range(t * ways, (t + 1) * ways)
        if t == 0:
            widen(patterns, wide, first)
        cut(send, L_ROWS, wide, here)
        for d in here:
            send[d, L_ROWS + P_ROWS : SEND1, :] = rows
        for cp in range(4):
            send[t * ways : (t + 1) * ways, cp * QS : (cp + 1) * QS, :] = total[
                :, cp * R : (cp + 1) * R
            ].reshape(ways, QS, R)
        piece = pl.ds(t * ways, ways)
        outs.append(pltpu.make_async_copy(send.at[piece], send_out.at[piece], out_sems.at[t]))
        outs[-1].start()
    for copy in outs:
        copy.wait()


def side_kernel(
    owner, patterns_in, index_in, mask_in, table_in, par_source_in, par_index_in, par_mask_in,
    par_table_in, interp_in, angle_in,
    near_out, coupling_out, own_table_out, weights_out, extra_out,
    patterns, index, mask, table, par_source, par_index, par_mask, par_table, interp, angle, sems,
    near, coupling, own_table, weights, extra, out_sems,
    wide, table_t, par_t, spread, par_rows, block,
):
    copies = start_all(
        (
            (table_in, table),
            (par_table_in, par_table),
            (patterns_in, patterns),
            (index_in, index),
            (mask_in, mask),
            (par_source_in, par_source),
            (par_index_in, par_index),
            (par_mask_in, par_mask),
            (interp_in, interp),
            (angle_in, angle),
        ),
        sems,
    )
    me = lax.axis_index("box")
    twice = jnp.int32(0)
    for i in range(owner.shape[0]):
        for j in range(i):
            same = (owner[i] >> 1) == (owner[j] >> 1)
            twice = jnp.where(same & (owner[i] != owner[j]), 1, twice)

    for copy in copies:
        copy.wait()
    transpose_table(table, table_t)
    for c in range(2):
        for part in range(NPAD // LANES):
            for k in range(KS):
                own_table[c, part, k : k + 1, :] = table_t[c, part, pl.ds(me * KS + k, 1), :]

    @pl.when(twice > 0)
    def _():
        widen(patterns, block, 1 - first_parity(owner, me))
        cut(extra, 0, block, range(DEV))
        copy = pltpu.make_async_copy(extra, extra_out, out_sems.at[4])
        copy.start()
        copy.wait()

    chosen = (iota((QS, Q), 1) == me * QS + iota((QS, Q), 0)).astype(BF16)
    count = par_table.shape[1]
    for c in range(2):
        rows = lax.dot_general(
            chosen, par_table[c], (((1,), (1,)), ((), ())), preferred_element_type=F32
        )
        split(par_t, c, jnp.concatenate([rows, jnp.zeros((QS, NPAD - count), F32)], axis=1))
    slots, parents = par_source.shape
    here = iota((LANES, LANES), 0)
    source_here = (here & (DEV - 1)) * 2 + ((here >> 5) & 1)
    par_rows[0, 0:slots, 0:parents] = par_source[...].astype(F32)
    par_rows[1, 0:slots, 0:parents] = jnp.where(
        par_mask[...] > 0, par_index[...], NPAD - 1
    ).astype(F32)
    wanted = source_here.astype(F32)
    table_at = jnp.full((LANES, LANES), NPAD - 1, F32)
    for j in range(slots):
        table_at = jnp.where(
            par_rows[0, j : j + 1, :] == wanted, par_rows[1, j : j + 1, :], table_at
        )
    par_rows[0] = jnp.transpose(table_at)
    number = jnp.concatenate(
        [par_rows[0, pl.ds(p, DEV, stride=2), :] for p in range(2)], axis=0
    ).astype(jnp.int32)
    par_low, par_chunk = number & (LANES - 1), number >> 7
    par_imaginary = iota((parents, LANES), 1) >= parents
    for q in range(QS):
        got = [
            pick(lambda part: par_t[c, part, q : q + 1, :], par_low, par_chunk) for c in range(2)
        ]
        coupling[q] = jnp.where(par_imaginary, got[1], got[0]).astype(BF16)
    outs = start_all(((coupling, coupling_out), (own_table, own_table_out)), out_sems)

    cosine, sine = jnp.cos(angle[...]), jnp.sin(angle[...])
    smooth = interp[...].astype(F32)
    for b in range(8):
        weights[b * K : (b + 1) * K, 0:Q] = (smooth * cosine[b : b + 1, :]).astype(BF16)
        weights[b * K : (b + 1) * K, Q : 2 * Q] = (smooth * sine[b : b + 1, :]).astype(BF16)
    outs.append(pltpu.make_async_copy(weights, weights_out, out_sems.at[2]))
    outs[-1].start()

    for c in range(2):
        for b in range(BOX):
            wide[c, b * K : (b + 1) * K, :] = patterns[c, b].astype(F32)
    spread[:, 0 : index.shape[1]] = jnp.where(mask[...] > 0, index[...], NPAD - 1)
    lane = iota((BOX, LANES), 1)
    code = jnp.take_along_axis(spread[...], lane & (BOX - 1), axis=1, mode="promise_in_bounds")
    low, chunk = code & (LANES - 1), code >> 7
    imaginary = ((lane >> 4) & 1) == 1
    zero = jnp.zeros((BOX, LANES), F32)

    for g in range(K // 8):
        left, right = [], []
        for kk in range(8):
            k = g * 8 + kk
            got = [
                pick(lambda part: table_t[c, part, k : k + 1, :], low, chunk) for c in range(2)
            ]
            value = jnp.where(imaginary, got[1], got[0])
            value = jnp.where((lane >> 5) == kk % 4, value, 0.0)
            left.append(
                jnp.concatenate([value, zero] if kk < 4 else [zero, value], axis=1)
            )
            real, imag = [wide[c, pl.ds(k, BOX, stride=K), :] for c in range(2)]
            right.append(doubled(real, imag))
        total = jnp.dot(
            jnp.concatenate(left, axis=0).astype(BF16),
            jnp.concatenate(right, axis=0),
            preferred_element_type=F32,
        )
        for kk in range(8):
            for c in range(2):
                near[c, pl.ds(g * 8 + kk, BOX, stride=K), :] = total[
                    kk * BOX : (kk + 1) * BOX, c * R : (c + 1) * R
                ]
    outs.append(pltpu.make_async_copy(near, near_out, out_sems.at[3]))
    outs[-1].start()
    for copy in outs:
        copy.wait()


def doubled(real, imag):
    return jnp.concatenate(
        [
            jnp.concatenate([real, imag], axis=1),
            jnp.concatenate([-imag, real], axis=1),
        ],
        axis=0,
    ).astype(BF16)


def middle_kernel(
    owner, received, extra, coupling, table, send,
    sems, fields, lifted, moved, codes, there,
):
    def place(s, c, half, piece):
        for k in range(2):
            row = (2 * half + k) * FAR + s * 8
            fields[c, row : row + 8, :] = piece[8 * k : 8 * k + 8].astype(F32)

    pieces = [
        (c, half, c * KS * 8 + half * 16) for c in range(2) for half in range(KS // 2)
    ]
    seconds = []
    for s in range(owner.shape[0]):
        device = owner[s] >> 1
        seconds.append((owner[s] & 1) != first_parity(owner, device))
        for c, half, at in pieces:
            place(s, c, half, received[device, L_ROWS + at : L_ROWS + at + 16, :])

    @pl.when(functools.reduce(jnp.logical_or, seconds))
    def _():
        for s, second in enumerate(seconds):

            @pl.when(second)
            def _():
                for c, half, at in pieces:
                    copy = pltpu.make_async_copy(
                        extra.at[owner[s] >> 1, at : at + 16], there, sems.at[0]
                    )
                    copy.start()
                    copy.wait()
                    place(s, c, half, there[...])

    size = DEV * QS
    for cp in range(4):
        lifted[cp * size : (cp + 1) * size, :] = (
            received[:, cp * QS : (cp + 1) * QS, :].reshape(size, R).astype(F32)
        )
    for q in range(QS):
        parts = [lifted[pl.ds(cp * size + q, DEV, stride=QS), :] for cp in range(4)]
        right = doubled(
            jnp.concatenate(parts[:2], axis=0), jnp.concatenate(parts[2:], axis=0)
        )
        total = jnp.dot(coupling[q], right, preferred_element_type=F32)
        for c in range(2):
            for p in range(2):
                moved[pl.ds((2 * c + p) * size + q, DEV, stride=QS), :] = total[
                    p * DEV : (p + 1) * DEV, c * R : (c + 1) * R
                ]
    for cp in range(4):
        send[:, cp * QS : (cp + 1) * QS, :] = (
            moved[cp * size : (cp + 1) * size, :].reshape(DEV, QS, R).astype(BF16)
        )

    codes[...] = (
        received[:, L_ROWS + P_ROWS : SEND1, :].reshape(DEV * BOX, LANES).astype(F32)
    )
    code = jnp.concatenate([codes[pl.ds(i, DEV, stride=BOX), :] for i in range(4)], axis=0)
    chunk = (code >= 32768.0).astype(jnp.int32) + (code >= 8388608.0).astype(jnp.int32)
    scale = jnp.where(chunk == 0, 1.0, jnp.where(chunk == 1, 1 / 256, 1 / 65536)).astype(F32)
    low = (code * scale).astype(jnp.int32) - 128
    low = low & (LANES - 1)
    lane = iota((4 * DEV, 2 * LANES), 1) & (LANES - 1)
    keeps = [jnp.where(lane >> 5 == group, 1.0, 0.0).astype(BF16) for group in range(4)]
    for k in range(KS):
        got = [
            pick(lambda part: table[c, part, k : k + 1, :], low, chunk) for c in range(2)
        ]
        both = jnp.concatenate(got, axis=1).astype(BF16)
        left = jnp.concatenate([both * keep for keep in keeps], axis=0)
        rows = slice(k * FAR, (k + 1) * FAR)
        right = doubled(
            jnp.concatenate([fields[0, rows, :]] * 4, axis=0),
            jnp.concatenate([fields[1, rows, :]] * 4, axis=0),
        )
        total = jnp.dot(left, right, preferred_element_type=F32)
        for c in range(2):
            for b in range(BOX):
                moved[pl.ds((4 + c * KS + k) * size + b, DEV, stride=BOX), :] = total[
                    b * DEV : (b + 1) * DEV, c * R : (c + 1) * R
                ]
    for ck in range(2 * KS):
        row = L_ROWS + ck * BOX
        send[:, row : row + BOX, :] = (
            moved[(4 + ck) * size : (5 + ck) * size, :].reshape(DEV, BOX, R).astype(BF16)
        )


def down_kernel(received, near, weights, out, fields, far, result, sems):
    for p in range(2):
        real = received[:, p * QS : (p + 1) * QS, :].reshape(Q, R)
        imag = received[:, (2 + p) * QS : (3 + p) * QS, :].reshape(Q, R)
        fields[0:Q, p * R : (p + 1) * R] = real
        fields[Q : 2 * Q, p * R : (p + 1) * R] = imag
        fields[0:Q, (2 + p) * R : (3 + p) * R] = imag
        fields[Q : 2 * Q, (2 + p) * R : (3 + p) * R] = -real
    for c in range(2):
        row = L_ROWS + c * KS * BOX
        far[c] = received[:, row : row + KS * BOX, :].reshape(K * BOX, R).astype(F32)
    copies = []
    for first in range(0, 8, GROUP):
        total = jnp.dot(
            weights[first * K : (first + GROUP) * K, :], fields[...], preferred_element_type=F32
        )
        for p in range(2):
            for b in range(first, first + GROUP):
                box = 8 * p + b
                for c in range(2):
                    there = far[c, pl.ds(box, K, stride=BOX), :]
                    at = (2 * c + p) * R
                    result[c, box] = (
                        total[(b - first) * K : (b - first + 1) * K, at : at + R]
                        + near[c, box * K : (box + 1) * K, :]
                        + there
                    )
        for p in range(2):
            boxes = pl.ds(8 * p + first, GROUP)
            copy = pltpu.make_async_copy(
                result.at[:, boxes], out.at[:, boxes], sems.at[2 * first + p]
            )
            copy.start()
            copies.append(copy)
    for copy in copies:
        copy.wait()


def in_vmem(count):
    return [pl.BlockSpec(memory_space=pltpu.VMEM)] * count


IN_HBM = pl.BlockSpec(memory_space=pltpu.HBM)
SCALARS = pl.BlockSpec(memory_space=pltpu.SMEM)


def anywhere(count):
    return [pl.BlockSpec(memory_space=pl.ANY)] * count


def params(limit):
    return pltpu.CompilerParams(vmem_limit_bytes=limit)


def shards(
    patterns,
    owner_block,
    low_index,
    low_mask,
    low_table,
    interp,
    shift_angle,
    par_source,
    par_index,
    par_mask,
    par_table,
):
    assert patterns.shape == (2, BOX, K, R) and interp.shape == (K, Q)
    assert lax.axis_size("box") == DEV and low_index.shape == (BOX, BOX + FAR)
    send = pl.pallas_call(
        up_kernel,
        out_shape=jax.ShapeDtypeStruct((DEV, SEND1, R), BF16),
        in_specs=anywhere(6),
        out_specs=IN_HBM,
        scratch_shapes=[
            pltpu.SMEM(owner_block.shape, jnp.int32),
            pltpu.VMEM(patterns.shape, BF16),
            pltpu.VMEM(low_index.shape, jnp.int32),
            pltpu.VMEM(low_mask.shape, jnp.int32),
            pltpu.VMEM(interp.shape, BF16),
            pltpu.VMEM(shift_angle.shape, F32),
            pltpu.SemaphoreType.DMA((6,)),
            pltpu.VMEM((16 * K, Q), BF16),
            pltpu.VMEM((16 * K, 4 * R), BF16),
            pltpu.VMEM((2, 8 * K, R), F32),
            pltpu.VMEM((BOX, LANES), jnp.int32),
            pltpu.VMEM((DEV, SEND1, R), BF16),
            pltpu.SemaphoreType.DMA((5,)),
        ],
        compiler_params=params(FULL),
        cost_estimate=pl.CostEstimate(
            flops=1200000000, bytes_accessed=4000000, transcendentals=8192
        ),
        name="up",
    )(owner_block, patterns, low_index, low_mask, interp, shift_angle)

    received = lax.all_to_all(send, "box", split_axis=0, concat_axis=0, tiled=True)

    made = (
        jax.ShapeDtypeStruct((2, BOX * K, R), F32),
        jax.ShapeDtypeStruct((QS, 2 * DEV, LANES), BF16),
        jax.ShapeDtypeStruct((2, NPAD // LANES, 8, LANES), F32),
        jax.ShapeDtypeStruct((8 * K, 2 * Q), BF16),
        jax.ShapeDtypeStruct((DEV, P_ROWS, R), BF16),
    )
    turned = [jnp.transpose(x) for x in (par_source, par_index, par_mask)]
    near, coupling, own_table, weights, extra = pl.pallas_call(
        side_kernel,
        out_shape=made,
        in_specs=[SCALARS, *anywhere(10)],
        out_specs=(IN_HBM,) * 5,
        scratch_shapes=[
            pltpu.VMEM(patterns.shape, BF16),
            pltpu.VMEM(low_index.shape, jnp.int32),
            pltpu.VMEM(low_mask.shape, jnp.int32),
            pltpu.VMEM(low_table.shape, BF16),
            *[pltpu.VMEM(x.shape, jnp.int32) for x in turned],
            pltpu.VMEM(par_table.shape, BF16),
            pltpu.VMEM(interp.shape, BF16),
            pltpu.VMEM(shift_angle.shape, F32),
            pltpu.SemaphoreType.DMA((10,)),
            *[pltpu.VMEM(x.shape, x.dtype) for x in made],
            pltpu.SemaphoreType.DMA((5,)),
            pltpu.VMEM((2, BOX * K, R), F32),
            pltpu.VMEM((2, NPAD // LANES, K, LANES), F32),
            pltpu.VMEM((2, NPAD // LANES, QS, LANES), F32),
            pltpu.VMEM((BOX, LANES), jnp.int32),
            pltpu.VMEM((2, LANES, LANES), F32),
            pltpu.VMEM((2, 8 * K, R), F32),
        ],
        compiler_params=params(FULL),
        cost_estimate=pl.CostEstimate(
            flops=4000000000, bytes_accessed=12000000, transcendentals=8192
        ),
        name="side",
    )(
        owner_block, patterns, low_index, low_mask, low_table, *turned, par_table, interp,
        shift_angle,
    )

    home, block = owner_block >> 1, owner_block
    twice = jnp.any((home[:, None] == home[None]) & (block[:, None] != block[None]))
    received, extra, twice = lax.optimization_barrier((received, extra, twice))
    extra = lax.cond(
        twice,
        lambda x: lax.all_to_all(x, "box", split_axis=0, concat_axis=0, tiled=True),
        lambda x: x,
        extra,
    )

    size = DEV * QS
    send = pl.pallas_call(
        middle_kernel,
        out_shape=jax.ShapeDtypeStruct((DEV, SEND2, R), BF16),
        in_specs=[SCALARS] + in_vmem(1) + anywhere(1) + in_vmem(2),
        out_specs=in_vmem(1)[0],
        scratch_shapes=[
            pltpu.SemaphoreType.DMA((1,)),
            pltpu.VMEM((2, KS * FAR, R), F32),
            pltpu.VMEM((4 * size, R), F32),
            pltpu.VMEM(((4 + 2 * KS) * size, R), F32),
            pltpu.VMEM((size, LANES), F32),
            pltpu.VMEM((16, R), BF16),
        ],
        compiler_params=params(LIMIT),
        cost_estimate=pl.CostEstimate(
            flops=800000000, bytes_accessed=4000000, transcendentals=0
        ),
        name="middle",
    )(owner_block, received, extra, coupling, own_table)

    received = lax.all_to_all(send, "box", split_axis=0, concat_axis=0, tiled=True)

    return pl.pallas_call(
        down_kernel,
        out_shape=jax.ShapeDtypeStruct((2, BOX, K, R), F32),
        in_specs=in_vmem(3),
        out_specs=IN_HBM,
        scratch_shapes=[
            pltpu.VMEM((2 * Q, 4 * R), BF16),
            pltpu.VMEM((2, K * BOX, R), F32),
            pltpu.VMEM((2, BOX, K, R), F32),
            pltpu.SemaphoreType.DMA((BOX,)),
        ],
        compiler_params=params(LIMIT),
        cost_estimate=pl.CostEstimate(
            flops=1200000000, bytes_accessed=6000000, transcendentals=0
        ),
        name="down",
    )(received, near, weights)


def solution(mesh):
    placed = (
        P(None, "box", None, "illum"),
        P(),
        P("box", None),
        P("box", None),
        P(),
        P(),
        P(),
        P(),
        P(),
        P(),
        P(),
    )
    return jax.shard_map(
        shards, mesh=mesh, in_specs=placed, out_specs=P(None, "box", None, "illum"), check_vma=False
    )
```

```python
import functools

import jax
import jax.numpy as jnp
from jax import lax
from jax.experimental import pallas as pl
from jax.experimental.pallas import tpu as pltpu
from jax.sharding import PartitionSpec as P

F32 = jnp.float32
BF16 = jnp.bfloat16
LANES = 128
LIMIT = 40 * 1024 * 1024
FULL = 60 * 1024 * 1024
GROUP = 1
DEV = 32
BOX = 16
K = 128
Q = 512
R = 128
QS = Q // DEV
KS = K // DEV
NPAD = 384
FAR = 32
L_ROWS = 4 * QS
P_ROWS = 2 * KS * 8
T_ROWS = BOX
SEND1 = L_ROWS + P_ROWS + T_ROWS
N_ROWS = 2 * KS * BOX
SEND2 = L_ROWS + N_ROWS


def iota(shape, dim):
    return lax.broadcasted_iota(jnp.int32, shape, dim)


def pick(row, index, chunk):
    total = None
    for part in range(NPAD // LANES):
        source = jnp.broadcast_to(row(part), index.shape)
        got = jnp.take_along_axis(source, index, axis=1, mode="promise_in_bounds")
        total = got if total is None else jnp.where(chunk == part, got, total)
    return total


def split(out_ref, c, rows):
    for part in range(NPAD // LANES):
        out_ref[c, part] = rows[:, part * LANES : (part + 1) * LANES]


def transpose_table(table_ref, out_ref):
    count = table_ref.shape[1]
    for part in range(2):
        wide = table_ref[part].astype(F32)
        wide = jnp.concatenate([wide, jnp.zeros((NPAD - count, wide.shape[1]), F32)], axis=0)
        split(out_ref, part, jnp.transpose(wide))


def first_parity(owner, device):
    result = jnp.int32(0)
    for step in reversed(range(owner.shape[0])):
        value = owner[step]
        result = jnp.where((value >> 1) == device, value & 1, result)
    return result


def widen(patterns, wide, parity):
    for c in range(2):
        for i in range(8):
            wide[c, i * K : (i + 1) * K, :] = patterns[c, parity * 8 + i].astype(F32)


def cut(out, base, wide, devices):
    for d in devices:
        for c in range(2):
            for half in range(KS // 2):
                pieces = [wide[c, pl.ds(d * KS + 2 * half + k, 8, stride=K), :] for k in range(2)]
                at = base + c * KS * 8 + half * 16
                out[d, at : at + 16, :] = jnp.concatenate(pieces, axis=0).astype(BF16)


def start_all(pairs, sems):
    copies = [pltpu.make_async_copy(*pair, sems.at[i]) for i, pair in enumerate(pairs)]
    for copy in copies:
        copy.start()
    return copies


def up_kernel(
    owner_in, patterns_in, index_in, mask_in, interp_in, angle_in, send_out,
    owner, patterns, index, mask, interp, angle, sems, weights, fields, wide, spread, send, out_sems,
):
    copies = start_all(
        (
            (interp_in, interp),
            (angle_in, angle),
            (patterns_in, patterns),
            (owner_in, owner),
            (index_in, index),
            (mask_in, mask),
        ),
        sems,
    )
    me = lax.axis_index("box")
    copies[0].wait()
    copies[1].wait()
    smooth = interp[...].astype(F32)
    cosine, sine = jnp.cos(angle[...]), jnp.sin(angle[...])
    for b in range(8):
        rows = 2 * b * K
        weights[rows : rows + K, :] = (smooth * cosine[b : b + 1, :]).astype(BF16)
        weights[rows + K : rows + 2 * K, :] = (smooth * sine[b : b + 1, :]).astype(BF16)
    for copy in copies[2:]:
        copy.wait()
    for b in range(8):
        rows = 2 * b * K
        for p in range(2):
            real, imag = patterns[0, 8 * p + b], patterns[1, 8 * p + b]
            fields[rows : rows + K, p * R : (p + 1) * R] = real
            fields[rows + K : rows + 2 * K, p * R : (p + 1) * R] = -imag
            fields[rows : rows + K, (2 + p) * R : (3 + p) * R] = imag
            fields[rows + K : rows + 2 * K, (2 + p) * R : (3 + p) * R] = real
    first = first_parity(owner, me)
    widen(patterns, wide, first)

    spread[:, 0 : index.shape[1]] = jnp.where(mask[...] > 0, index[...], NPAD - 1)
    lane = iota((BOX, LANES), 1)
    number = jnp.take_along_axis(
        spread[...], BOX + (lane & (FAR - 1)), axis=1, mode="promise_in_bounds"
    )
    chunk = number >> 7
    scale = jnp.where(chunk == 0, 1.0, jnp.where(chunk == 1, 256.0, 65536.0)).astype(F32)
    code = ((number & (LANES - 1)) + 128).astype(F32) * scale
    quarter = BOX // 4
    packed = code[0:quarter]
    for group in range(1, 4):
        packed = jnp.where(
            lane[0:quarter] >> 5 == group, code[group * quarter : (group + 1) * quarter], packed
        )
    rows = jnp.concatenate([packed] * 4, axis=0).astype(BF16)
    tile = 256
    ways = tile // QS
    outs = []
    for t in range(Q // tile):
        total = lax.dot_general(
            weights[:, t * tile : (t + 1) * tile],
            fields[...],
            (((0,), (0,)), ((), ())),
            preferred_element_type=F32,
        ).astype(BF16)
        here = range(t * ways, (t + 1) * ways)
        cut(send, L_ROWS, wide, here)
        for d in here:
            send[d, L_ROWS + P_ROWS : SEND1, :] = rows
        for cp in range(4):
            send[t * ways : (t + 1) * ways, cp * QS : (cp + 1) * QS, :] = total[
                :, cp * R : (cp + 1) * R
            ].reshape(ways, QS, R)
        piece = pl.ds(t * ways, ways)
        outs.append(pltpu.make_async_copy(send.at[piece], send_out.at[piece], out_sems.at[t]))
        outs[-1].start()
    for copy in outs:
        copy.wait()


def side_kernel(
    owner, patterns_in, index_in, mask_in, table_in, par_source_in, par_index_in, par_mask_in,
    par_table_in, interp_in, angle_in,
    near_out, coupling_out, own_table_out, weights_out, extra_out,
    patterns, index, mask, table, par_source, par_index, par_mask, par_table, interp, angle, sems,
    near, coupling, own_table, weights, extra, out_sems,
    wide, table_t, par_t, spread, par_rows, block,
):
    copies = start_all(
        (
            (table_in, table),
            (par_table_in, par_table),
            (patterns_in, patterns),
            (index_in, index),
            (mask_in, mask),
            (par_source_in, par_source),
            (par_index_in, par_index),
            (par_mask_in, par_mask),
            (interp_in, interp),
            (angle_in, angle),
        ),
        sems,
    )
    me = lax.axis_index("box")
    twice = jnp.int32(0)
    for i in range(owner.shape[0]):
        for j in range(i):
            same = (owner[i] >> 1) == (owner[j] >> 1)
            twice = jnp.where(same & (owner[i] != owner[j]), 1, twice)

    for copy in copies:
        copy.wait()
    transpose_table(table, table_t)
    for c in range(2):
        for part in range(NPAD // LANES):
            for k in range(KS):
                own_table[c, part, k : k + 1, :] = table_t[c, part, pl.ds(me * KS + k, 1), :]

    @pl.when(twice > 0)
    def _():
        widen(patterns, block, 1 - first_parity(owner, me))
        cut(extra, 0, block, range(DEV))
        copy = pltpu.make_async_copy(extra, extra_out, out_sems.at[4])
        copy.start()
        copy.wait()

    chosen = (iota((QS, Q), 1) == me * QS + iota((QS, Q), 0)).astype(BF16)
    count = par_table.shape[1]
    for c in range(2):
        rows = lax.dot_general(
            chosen, par_table[c], (((1,), (1,)), ((), ())), preferred_element_type=F32
        )
        split(par_t, c, jnp.concatenate([rows, jnp.zeros((QS, NPAD - count), F32)], axis=1))
    slots, parents = par_source.shape
    here = iota((LANES, LANES), 0)
    source_here = (here & (DEV - 1)) * 2 + ((here >> 5) & 1)
    par_rows[0, 0:slots, 0:parents] = par_source[...].astype(F32)
    par_rows[1, 0:slots, 0:parents] = jnp.where(
        par_mask[...] > 0, par_index[...], NPAD - 1
    ).astype(F32)
    wanted = source_here.astype(F32)
    table_at = jnp.full((LANES, LANES), NPAD - 1, F32)
    for j in range(slots):
        table_at = jnp.where(
            par_rows[0, j : j + 1, :] == wanted, par_rows[1, j : j + 1, :], table_at
        )
    par_rows[0] = jnp.transpose(table_at)
    number = jnp.concatenate(
        [par_rows[0, pl.ds(p, DEV, stride=2), :] for p in range(2)], axis=0
    ).astype(jnp.int32)
    par_low, par_chunk = number & (LANES - 1), number >> 7
    par_imaginary = iota((parents, LANES), 1) >= parents
    for q in range(QS):
        got = [
            pick(lambda part: par_t[c, part, q : q + 1, :], par_low, par_chunk) for c in range(2)
        ]
        coupling[q] = jnp.where(par_imaginary, got[1], got[0]).astype(BF16)
    outs = start_all(((coupling, coupling_out), (own_table, own_table_out)), out_sems)

    cosine, sine = jnp.cos(angle[...]), jnp.sin(angle[...])
    smooth = interp[...].astype(F32)
    for b in range(8):
        weights[b * K : (b + 1) * K, 0:Q] = (smooth * cosine[b : b + 1, :]).astype(BF16)
        weights[b * K : (b + 1) * K, Q : 2 * Q] = (smooth * sine[b : b + 1, :]).astype(BF16)
    outs.append(pltpu.make_async_copy(weights, weights_out, out_sems.at[2]))
    outs[-1].start()

    for c in range(2):
        for b in range(BOX):
            wide[c, b * K : (b + 1) * K, :] = patterns[c, b].astype(F32)
    spread[:, 0 : index.shape[1]] = jnp.where(mask[...] > 0, index[...], NPAD - 1)
    lane = iota((BOX, LANES), 1)
    code = jnp.take_along_axis(spread[...], lane & (BOX - 1), axis=1, mode="promise_in_bounds")
    low, chunk = code & (LANES - 1), code >> 7
    imaginary = ((lane >> 4) & 1) == 1
    zero = jnp.zeros((BOX, LANES), F32)

    for g in range(K // 8):
        left, right = [], []
        for kk in range(8):
            k = g * 8 + kk
            got = [
                pick(lambda part: table_t[c, part, k : k + 1, :], low, chunk) for c in range(2)
            ]
            value = jnp.where(imaginary, got[1], got[0])
            value = jnp.where((lane >> 5) == kk % 4, value, 0.0)
            left.append(
                jnp.concatenate([value, zero] if kk < 4 else [zero, value], axis=1)
            )
            real, imag = [wide[c, pl.ds(k, BOX, stride=K), :] for c in range(2)]
            right.append(doubled(real, imag))
        total = jnp.dot(
            jnp.concatenate(left, axis=0).astype(BF16),
            jnp.concatenate(right, axis=0),
            preferred_element_type=F32,
        )
        for kk in range(8):
            for c in range(2):
                near[c, pl.ds(g * 8 + kk, BOX, stride=K), :] = total[
                    kk * BOX : (kk + 1) * BOX, c * R : (c + 1) * R
                ]
    outs.append(pltpu.make_async_copy(near, near_out, out_sems.at[3]))
    outs[-1].start()
    for copy in outs:
        copy.wait()


def doubled(real, imag):
    return jnp.concatenate(
        [
            jnp.concatenate([real, imag], axis=1),
            jnp.concatenate([-imag, real], axis=1),
        ],
        axis=0,
    ).astype(BF16)


def middle_kernel(
    owner, received, extra, coupling, table, send,
    sems, fields, lifted, moved, codes, there,
):
    def place(s, c, half, piece):
        for k in range(2):
            row = (2 * half + k) * FAR + s * 8
            fields[c, row : row + 8, :] = piece[8 * k : 8 * k + 8].astype(F32)

    pieces = [
        (c, half, c * KS * 8 + half * 16) for c in range(2) for half in range(KS // 2)
    ]
    seconds = []
    for s in range(owner.shape[0]):
        device = owner[s] >> 1
        seconds.append((owner[s] & 1) != first_parity(owner, device))
        for c, half, at in pieces:
            place(s, c, half, received[device, L_ROWS + at : L_ROWS + at + 16, :])

    @pl.when(functools.reduce(jnp.logical_or, seconds))
    def _():
        for s, second in enumerate(seconds):

            @pl.when(second)
            def _():
                for c, half, at in pieces:
                    copy = pltpu.make_async_copy(
                        extra.at[owner[s] >> 1, at : at + 16], there, sems.at[0]
                    )
                    copy.start()
                    copy.wait()
                    place(s, c, half, there[...])

    size = DEV * QS
    for cp in range(4):
        lifted[cp * size : (cp + 1) * size, :] = (
            received[:, cp * QS : (cp + 1) * QS, :].reshape(size, R).astype(F32)
        )
    for q in range(QS):
        parts = [lifted[pl.ds(cp * size + q, DEV, stride=QS), :] for cp in range(4)]
        right = doubled(
            jnp.concatenate(parts[:2], axis=0), jnp.concatenate(parts[2:], axis=0)
        )
        total = jnp.dot(coupling[q], right, preferred_element_type=F32)
        for c in range(2):
            for p in range(2):
                moved[pl.ds((2 * c + p) * size + q, DEV, stride=QS), :] = total[
                    p * DEV : (p + 1) * DEV, c * R : (c + 1) * R
                ]
    for cp in range(4):
        send[:, cp * QS : (cp + 1) * QS, :] = (
            moved[cp * size : (cp + 1) * size, :].reshape(DEV, QS, R).astype(BF16)
        )

    codes[...] = (
        received[:, L_ROWS + P_ROWS : SEND1, :].reshape(DEV * BOX, LANES).astype(F32)
    )
    code = jnp.concatenate([codes[pl.ds(i, DEV, stride=BOX), :] for i in range(4)], axis=0)
    chunk = (code >= 32768.0).astype(jnp.int32) + (code >= 8388608.0).astype(jnp.int32)
    scale = jnp.where(chunk == 0, 1.0, jnp.where(chunk == 1, 1 / 256, 1 / 65536)).astype(F32)
    low = (code * scale).astype(jnp.int32) - 128
    low = low & (LANES - 1)
    lane = iota((4 * DEV, 2 * LANES), 1) & (LANES - 1)
    keeps = [jnp.where(lane >> 5 == group, 1.0, 0.0).astype(BF16) for group in range(4)]
    for k in range(KS):
        got = [
            pick(lambda part: table[c, part, k : k + 1, :], low, chunk) for c in range(2)
        ]
        both = jnp.concatenate(got, axis=1).astype(BF16)
        left = jnp.concatenate([both * keep for keep in keeps], axis=0)
        rows = slice(k * FAR, (k + 1) * FAR)
        right = doubled(
            jnp.concatenate([fields[0, rows, :]] * 4, axis=0),
            jnp.concatenate([fields[1, rows, :]] * 4, axis=0),
        )
        total = jnp.dot(left, right, preferred_element_type=F32)
        for c in range(2):
            for b in range(BOX):
                moved[pl.ds((c * KS + k) * size + b, DEV, stride=BOX), :] = total[
                    b * DEV : (b + 1) * DEV, c * R : (c + 1) * R
                ]
    for ck in range(2 * KS):
        row = L_ROWS + ck * BOX
        send[:, row : row + BOX, :] = (
            moved[ck * size : (ck + 1) * size, :].reshape(DEV, BOX, R).astype(BF16)
        )


def down_kernel(received, near, weights, out, fields, far, result, sems):
    for p in range(2):
        real = received[:, p * QS : (p + 1) * QS, :].reshape(Q, R)
        imag = received[:, (2 + p) * QS : (3 + p) * QS, :].reshape(Q, R)
        fields[0:Q, p * R : (p + 1) * R] = real
        fields[Q : 2 * Q, p * R : (p + 1) * R] = imag
        fields[0:Q, (2 + p) * R : (3 + p) * R] = imag
        fields[Q : 2 * Q, (2 + p) * R : (3 + p) * R] = -real
    for c in range(2):
        row = L_ROWS + c * KS * BOX
        far[c] = received[:, row : row + KS * BOX, :].reshape(K * BOX, R).astype(F32)
    copies = []
    for first in range(0, 8, GROUP):
        total = jnp.dot(
            weights[first * K : (first + GROUP) * K, :], fields[...], preferred_element_type=F32
        )
        for p in range(2):
            for b in range(first, first + GROUP):
                box = 8 * p + b
                for c in range(2):
                    there = far[c, pl.ds(box, K, stride=BOX), :]
                    at = (2 * c + p) * R
                    result[c, box] = (
                        total[(b - first) * K : (b - first + 1) * K, at : at + R]
                        + near[c, box * K : (box + 1) * K, :]
                        + there
                    )
        for p in range(2):
            boxes = pl.ds(8 * p + first, GROUP)
            copy = pltpu.make_async_copy(
                result.at[:, boxes], out.at[:, boxes], sems.at[2 * first + p]
            )
            copy.start()
            copies.append(copy)
    for copy in copies:
        copy.wait()


def in_vmem(count):
    return [pl.BlockSpec(memory_space=pltpu.VMEM)] * count


IN_HBM = pl.BlockSpec(memory_space=pltpu.HBM)
SCALARS = pl.BlockSpec(memory_space=pltpu.SMEM)


def anywhere(count):
    return [pl.BlockSpec(memory_space=pl.ANY)] * count


def params(limit):
    return pltpu.CompilerParams(vmem_limit_bytes=limit)


def shards(
    patterns,
    owner_block,
    low_index,
    low_mask,
    low_table,
    interp,
    shift_angle,
    par_source,
    par_index,
    par_mask,
    par_table,
):
    assert patterns.shape == (2, BOX, K, R) and interp.shape == (K, Q)
    assert lax.axis_size("box") == DEV and low_index.shape == (BOX, BOX + FAR)
    send = pl.pallas_call(
        up_kernel,
        out_shape=jax.ShapeDtypeStruct((DEV, SEND1, R), BF16),
        in_specs=anywhere(6),
        out_specs=IN_HBM,
        scratch_shapes=[
            pltpu.SMEM(owner_block.shape, jnp.int32),
            pltpu.VMEM(patterns.shape, BF16),
            pltpu.VMEM(low_index.shape, jnp.int32),
            pltpu.VMEM(low_mask.shape, jnp.int32),
            pltpu.VMEM(interp.shape, BF16),
            pltpu.VMEM(shift_angle.shape, F32),
            pltpu.SemaphoreType.DMA((6,)),
            pltpu.VMEM((16 * K, Q), BF16),
            pltpu.VMEM((16 * K, 4 * R), BF16),
            pltpu.VMEM((2, 8 * K, R), F32),
            pltpu.VMEM((BOX, LANES), jnp.int32),
            pltpu.VMEM((DEV, SEND1, R), BF16),
            pltpu.SemaphoreType.DMA((5,)),
        ],
        compiler_params=params(FULL),
        cost_estimate=pl.CostEstimate(
            flops=1200000000, bytes_accessed=4000000, transcendentals=8192
        ),
        name="up",
    )(owner_block, patterns, low_index, low_mask, interp, shift_angle)

    received = lax.all_to_all(send, "box", split_axis=0, concat_axis=0, tiled=True)

    made = (
        jax.ShapeDtypeStruct((2, BOX * K, R), F32),
        jax.ShapeDtypeStruct((QS, 2 * DEV, LANES), BF16),
        jax.ShapeDtypeStruct((2, NPAD // LANES, 8, LANES), F32),
        jax.ShapeDtypeStruct((8 * K, 2 * Q), BF16),
        jax.ShapeDtypeStruct((DEV, P_ROWS, R), BF16),
    )
    turned = [jnp.transpose(x) for x in (par_source, par_index, par_mask)]
    near, coupling, own_table, weights, extra = pl.pallas_call(
        side_kernel,
        out_shape=made,
        in_specs=[SCALARS, *anywhere(10)],
        out_specs=(IN_HBM,) * 5,
        scratch_shapes=[
            pltpu.VMEM(patterns.shape, BF16),
            pltpu.VMEM(low_index.shape, jnp.int32),
            pltpu.VMEM(low_mask.shape, jnp.int32),
            pltpu.VMEM(low_table.shape, BF16),
            *[pltpu.VMEM(x.shape, jnp.int32) for x in turned],
            pltpu.VMEM(par_table.shape, BF16),
            pltpu.VMEM(interp.shape, BF16),
            pltpu.VMEM(shift_angle.shape, F32),
            pltpu.SemaphoreType.DMA((10,)),
            *[pltpu.VMEM(x.shape, x.dtype) for x in made],
            pltpu.SemaphoreType.DMA((5,)),
            pltpu.VMEM((2, BOX * K, R), F32),
            pltpu.VMEM((2, NPAD // LANES, K, LANES), F32),
            pltpu.VMEM((2, NPAD // LANES, QS, LANES), F32),
            pltpu.VMEM((BOX, LANES), jnp.int32),
            pltpu.VMEM((2, LANES, LANES), F32),
            pltpu.VMEM((2, 8 * K, R), F32),
        ],
        compiler_params=params(FULL),
        cost_estimate=pl.CostEstimate(
            flops=4000000000, bytes_accessed=12000000, transcendentals=8192
        ),
        name="side",
    )(
        owner_block, patterns, low_index, low_mask, low_table, *turned, par_table, interp,
        shift_angle,
    )

    home, block = owner_block >> 1, owner_block
    twice = jnp.any((home[:, None] == home[None]) & (block[:, None] != block[None]))
    received, extra, twice = lax.optimization_barrier((received, extra, twice))
    extra = lax.cond(
        twice,
        lambda x: lax.all_to_all(x, "box", split_axis=0, concat_axis=0, tiled=True),
        lambda x: x,
        extra,
    )

    size = DEV * QS
    send = pl.pallas_call(
        middle_kernel,
        out_shape=jax.ShapeDtypeStruct((DEV, SEND2, R), BF16),
        in_specs=[SCALARS] + in_vmem(1) + anywhere(1) + in_vmem(2),
        out_specs=in_vmem(1)[0],
        scratch_shapes=[
            pltpu.SemaphoreType.DMA((1,)),
            pltpu.VMEM((2, KS * FAR, R), F32),
            pltpu.VMEM((4 * size, R), F32),
            pltpu.VMEM((2 * KS * size, R), F32),
            pltpu.VMEM((size, LANES), F32),
            pltpu.VMEM((16, R), BF16),
        ],
        compiler_params=params(LIMIT),
        cost_estimate=pl.CostEstimate(
            flops=800000000, bytes_accessed=4000000, transcendentals=0
        ),
        name="middle",
    )(owner_block, received, extra, coupling, own_table)

    received = lax.all_to_all(send, "box", split_axis=0, concat_axis=0, tiled=True)

    return pl.pallas_call(
        down_kernel,
        out_shape=jax.ShapeDtypeStruct((2, BOX, K, R), F32),
        in_specs=in_vmem(3),
        out_specs=IN_HBM,
        scratch_shapes=[
            pltpu.VMEM((2 * Q, 4 * R), BF16),
            pltpu.VMEM((2, K * BOX, R), F32),
            pltpu.VMEM((2, BOX, K, R), F32),
            pltpu.SemaphoreType.DMA((BOX,)),
        ],
        compiler_params=params(LIMIT),
        cost_estimate=pl.CostEstimate(
            flops=1200000000, bytes_accessed=6000000, transcendentals=0
        ),
        name="down",
    )(received, near, weights)


def solution(mesh):
    placed = (
        P(None, "box", None, "illum"),
        P(),
        P("box", None),
        P("box", None),
        P(),
        P(),
        P(),
        P(),
        P(),
        P(),
        P(),
    )
    return jax.shard_map(
        shards, mesh=mesh, in_specs=placed, out_specs=P(None, "box", None, "illum"), check_vma=False
    )
```
